32 devices in a mesh: brick: 8 (over z, y), pencil: 4 (over x, core).
Axes of the slice: x: 2, y: 2, z: 4, core: 2. Of those that a mesh axis runs over, the one named last changes fastest.
Arguments:
- positions: float32 [3, 131072], P(None, ('brick', 'pencil')), may hold values from 3 to 16, as said below
- charges: float32 [131072], P(('brick', 'pencil')), may hold values from -2.5 to 2.5
- anchor_row: int32 [2048], P(('brick', 'pencil')), may hold values from 0 to 115
- anchor_column: int32 [2048], P(('brick', 'pencil')), may hold values from 0 to 511
- counts: int32 [32], P(('brick', 'pencil')), may hold values from 16 to 64, as said below
Outputs:
- energy: float32 [1], replicated
- spectrum: float32 [2, 24, 512, 512], P(None, None, 'brick', 'pencil')
The draws below stay inside these ranges and needn't reach their ends.
Inputs may be any that keep to these rules, and one draw needn't show every extreme that they name: positions[0] lies in 3 to 6, positions[1] in 3 to 16, positions[2] in 3 to 16. counts[d] is the number of live blocks of device d, the first ones of its slots; 64 is reached on some devices in every draw.
All inputs are finite; a program needn't handle non-finite values.
Results may differ from the reference program's by a relative error of at most 0.0025.
Values sent between devices are 32-bit elements; how exact they have to be, the bound alone decides.
A program may use at most 64 MiB of HBM per device.

```python
import math
import jax
import jax.numpy as jnp
from jax import lax

NX = 512
NY = 512
ZDEV = 3
BCAP = 64
BLOCK_ATOMS = 64
PY = 16
PX = 16
NZ = 24
BLOCKS = 2048
ATOMS = 131072
N_PENCIL = 4
DEVICES = 32


def draw_positions(key, part):
    split_keys = jax.random.split(key, 3)
    upper_ends = [ZDEV + 3.0, PY * 1.0, PX * 1.0]
    coordinate_rows = []
    for component in range(3):
        uniform_value = jax.random.uniform(split_keys[component], (ATOMS,), jnp.float32)
        coordinate_rows.append(3.0 + (upper_ends[component] - 3.0) * uniform_value)
    return jnp.stack(coordinate_rows)


def draw_charges(key, part):
    key_two = jax.random.fold_in(key, 1)
    return jnp.clip(0.5 * jax.random.normal(key_two, (ATOMS,), jnp.float32), -2.5, 2.5)


def draw_counts(key, part):
    key_one, key_two = jax.random.split(key)
    base_counts = jax.random.randint(key_one, (DEVICES,), BCAP // 4, 3 * BCAP // 4 + 1)
    chosen = jax.random.permutation(key_two, DEVICES)[:4]
    return base_counts.at[chosen].set(BCAP).astype(jnp.int32)


def with_ends(array, rng, low, top_value):
    longest = array.shape.index(max(array.shape))
    spots = []
    for shift in (0, 1):
        where = [jax.random.randint(jax.random.fold_in(rng, axis), (), 0, length) for axis, length in enumerate(array.shape)]
        where[longest] = (where[longest] + shift) % array.shape[longest]
        spots.append(tuple(where))
    return array.at[spots[0]].set(low).at[spots[1]].set(top_value)


def setup_inputs(seed: int = 0) -> dict:
    arg_keys = jax.random.split(jax.random.key(seed), 6)
    return {
        "positions": draw_positions(jax.random.fold_in(arg_keys[5], 71), 0),
        "charges": draw_charges(jax.random.fold_in(arg_keys[5], 71), 0),
        "anchor_row": with_ends(jax.random.randint(arg_keys[2], (BLOCKS,), 0, NY // N_PENCIL - PY + 4), jax.random.fold_in(arg_keys[2], 1), 0, (NY // N_PENCIL - PY + 4) - 1).astype(jnp.int32),
        "anchor_column": with_ends(jax.random.randint(arg_keys[3], (BLOCKS,), 0, NX), jax.random.fold_in(arg_keys[3], 1), 0, NX - 1).astype(jnp.int32),
        "counts": draw_counts(jax.random.fold_in(arg_keys[5], 71), 0),
    }


FULL_TURN = 2.0 * math.pi
EWALD_SPLIT = 0.35
HIGHEST = lax.Precision.HIGHEST


def spline(offset):
    distance = jnp.abs(offset - 2.0)
    inner_part = (4.0 - 6.0 * distance * distance + 3.0 * distance * distance * distance) / 6.0
    remain = 2.0 - distance
    outer_part = remain * remain * remain / 6.0
    return jnp.where(distance < 1.0, inner_part, jnp.where(distance < 2.0, outer_part, 0.0))


def patches(coords, charge, patch_depth, patch_rows, patch_columns):
    blocks_here = coords.shape[1]
    atoms_here = coords.shape[2]
    weight_depth = spline(coords[0][:, :, None] - jnp.arange(patch_depth, dtype=jnp.float32)) * charge[:, :, None]
    weight_rows = spline(coords[1][:, :, None] - jnp.arange(patch_rows, dtype=jnp.float32))
    weight_columns = spline(coords[2][:, :, None] - jnp.arange(patch_columns, dtype=jnp.float32))
    sheet = (weight_rows[:, :, :, None] * weight_columns[:, :, None, :]).reshape(blocks_here, atoms_here, patch_rows * patch_columns)
    return jnp.einsum("gaz,gak->gzk", weight_depth, sheet, precision=HIGHEST)


def terms_of(wave_index, length):
    signed = jnp.where(2 * wave_index >= length, wave_index - length, wave_index)
    fraction = signed.astype(jnp.float32) / length
    cosine = jnp.cos(wave_index.astype(jnp.float32) * (FULL_TURN / length))
    spline_fix = 9.0 / ((2.0 + cosine) * (2.0 + cosine))
    return fraction * fraction, spline_fix


def ewald_kernel(z_terms, y_terms, x_terms, length):
    squared = z_terms[0][:, None, None] + y_terms[0][None, :, None] + x_terms[0][None, None, :]
    anchor = squared == 0.0
    safe_squared = jnp.where(anchor, 1.0, squared)
    damped = jnp.exp(squared * (-(math.pi * math.pi) / (EWALD_SPLIT * EWALD_SPLIT))) / (safe_squared * (math.pi * (length * NY * NX)))
    fixes = z_terms[1][:, None, None] * y_terms[1][None, :, None] * x_terms[1][None, None, :]
    return jnp.where(anchor, 0.0, damped) * fixes


def reference(positions, charges, anchor_row, anchor_column, counts):
    pencil_rows = NY // N_PENCIL
    patch_depth = ZDEV + 3
    coords = positions.reshape(3, DEVICES, BCAP, BLOCK_ATOMS)
    charge = charges.reshape(DEVICES, BCAP, BLOCK_ATOMS)
    anchor_rows = anchor_row.reshape(DEVICES, BCAP)
    anchor_columns = anchor_column.reshape(DEVICES, BCAP)
    slot_index = jnp.arange(BCAP, dtype=jnp.int32)
    plane_steps = jnp.arange(patch_depth, dtype=jnp.int32)
    line_index = jnp.arange(PY, dtype=jnp.int32)
    cell_index = jnp.arange(PX, dtype=jnp.int32)

    def add_device(device, charge_grid):
        device = device.astype(jnp.int32)
        slab_index = device // N_PENCIL
        quarter = device % N_PENCIL
        live_mask = (slot_index < counts[device]).astype(jnp.float32)
        values = patches(coords[:, device], charge[device] * live_mask[:, None], patch_depth, PY, PX)
        plane_index = (slab_index * ZDEV + plane_steps - 3) % NZ
        row_index = (quarter * pencil_rows + anchor_rows[device][:, None] + line_index - 3) % NY
        column_index = (anchor_columns[device][:, None] + cell_index) % NX
        flat_index = (plane_index[None, :, None, None] * NY + row_index[:, None, :, None]) * NX + column_index[:, None, None, :]
        return charge_grid.at[flat_index.reshape(-1)].add(values.reshape(-1))

    charge_grid = lax.fori_loop(0, DEVICES, add_device, jnp.zeros(NZ * NY * NX, jnp.float32))
    transformed = jnp.fft.fftn(charge_grid.reshape(NZ, NY, NX))
    stacked = jnp.stack([jnp.real(transformed), jnp.imag(transformed)]).astype(jnp.float32)
    kernel = ewald_kernel(terms_of(jnp.arange(NZ, dtype=jnp.int32), NZ), terms_of(jnp.arange(NY, dtype=jnp.int32), NY), terms_of(jnp.arange(NX, dtype=jnp.int32), NX), NZ)
    power = stacked[0] * stacked[0] + stacked[1] * stacked[1]
    energy = (0.5 / BLOCKS) * jnp.sum(kernel * power)
    return (energy.reshape(1).astype(jnp.float32), stacked)
```

```python
import functools
import math

import jax
import jax.numpy as jnp
import numpy as np
from jax import lax
from jax.experimental import pallas as pl
from jax.experimental.pallas import tpu as pltpu
from jax.sharding import PartitionSpec as P

NX = 512
NY = 512
ZDEV = 3
PY = 16
PX = 16
LANES = 128
RIM = 8
GROUP = 4

FULL_TURN = 2.0 * math.pi
EWALD_SPLIT = 0.35
HIGH = lax.Precision.HIGH


def from_behind(block, axis, distance):
    devices = range(lax.axis_size(axis))
    route = [((i - distance) % len(devices), i) for i in devices]
    return lax.ppermute(block, axis, route)


def spline(offset):
    distance = jnp.abs(offset - 2.0)
    outer = jnp.maximum(2.0 - distance, 0.0)
    inner = jnp.maximum(1.0 - distance, 0.0)
    return (outer * outer * outer - 4.0 * (inner * inner * inner)) * (1.0 / 6.0)


def split(value):
    high = value.astype(jnp.bfloat16)
    low = (value - high.astype(jnp.float32)).astype(jnp.bfloat16)
    return high, low


def dot3(left, right, dims):
    def one(a, b):
        return lax.dot_general(a, b, (dims, ((), ())), preferred_element_type=jnp.float32)

    return one(left[0], right[1]) + one(left[1], right[0]) + one(left[0], right[0])


def spread_kernel(first_plane, block_atoms, *refs):
    row_ref, column_ref, coords_ref, charge_ref, *before, grid_ref = refs
    slots = row_ref.shape[0]
    if before:
        grid_ref[...] = before[0][...]
    else:
        grid_ref[...] = jnp.zeros_like(grid_ref)
    tiles = grid_ref.shape[0]
    width = GROUP * block_atoms
    lane_block = lax.broadcasted_iota(jnp.int32, (PY, width), 1) // block_atoms
    steps = lax.broadcasted_iota(jnp.int32, (PY, width), 0).astype(jnp.float32)
    planes = (lax.broadcasted_iota(jnp.int32, (8, width), 0) + first_plane).astype(jnp.float32)
    lane = lax.broadcasted_iota(jnp.int32, (ZDEV * PY, LANES), 1)
    blank = jnp.zeros((LANES - PX, width), jnp.bfloat16)

    def turn(step, carry):
        here = pl.ds(pl.multiple_of(step * width, width), width)
        depth = spline(coords_ref[0:1, here] - planes) * charge_ref[0:1, here]
        lines = spline(coords_ref[1:2, here] - steps)
        cells = split(spline(coords_ref[2:3, here] - steps))
        cells = [jnp.concatenate([part, blank], axis=0) for part in cells]
        pieces = []
        for member in range(GROUP):
            own = jnp.where(lane_block == member, lines, 0.0)
            for plane in range(ZDEV):
                pieces.append(split(own * depth[plane : plane + 1]))
        sheets = [jnp.concatenate([piece[i] for piece in pieces], axis=0) for i in range(2)]
        values = dot3(sheets, cells, ((1,), (1,)))
        for member in range(GROUP):
            block = step * GROUP + member
            column = column_ref[block]
            row = row_ref[block] + (RIM - 3)
            shift = column & (LANES - 1)
            tile = column // LANES
            over = (tile + 1) & (tiles - 1)
            patch = values[member * ZDEV * PY : (member + 1) * ZDEV * PY]
            patch = pltpu.roll(patch, shift, 1)
            parts = (
                (tile, jnp.where(lane >= shift, patch, 0.0)),
                (over, jnp.where(lane >= shift, 0.0, patch)),
            )
            sums = []
            for where, part in parts:
                for plane in range(ZDEV):
                    old = grid_ref[where, plane, pl.ds(row, PY), :]
                    sums.append(old + part[plane * PY : (plane + 1) * PY])
            for index, (where, part) in enumerate(parts):
                for plane in range(ZDEV):
                    grid_ref[where, plane, pl.ds(row, PY), :] = sums[index * ZDEV + plane]
        return carry

    lax.fori_loop(0, slots // GROUP, turn, 0)


def spread(first_plane, rows, anchor_row, anchor_column, coords, charge, *before):
    slots = anchor_row.shape[0]
    shape = (NX // LANES, ZDEV, rows + RIM, LANES)
    scalar = pl.BlockSpec(memory_space=pltpu.SMEM)
    whole = pl.BlockSpec(memory_space=pltpu.VMEM)
    return pl.pallas_call(
        functools.partial(spread_kernel, first_plane, charge.shape[1] // slots),
        out_shape=jax.ShapeDtypeStruct(shape, jnp.float32),
        in_specs=[scalar, scalar] + [whole] * (2 + len(before)),
        out_specs=whole,
        compiler_params=pltpu.CompilerParams(vmem_limit_bytes=24 * 1024 * 1024),
        cost_estimate=pl.CostEstimate(
            flops=20_000_000, bytes_accessed=4_000_000, transcendentals=0
        ),
    )(anchor_row, anchor_column, coords, charge, *before)


def terms_of(wave_index, length):
    signed = jnp.where(2 * wave_index >= length, wave_index - length, wave_index)
    fraction = signed.astype(jnp.float32) / length
    cosine = jnp.cos(wave_index.astype(jnp.float32) * (FULL_TURN / length))
    spline_fix = 9.0 / ((2.0 + cosine) * (2.0 + cosine))
    return (fraction * fraction, spline_fix)


def ewald_kernel(z_terms, y_terms, x_terms, length):
    squared = z_terms[0][:, None, None] + y_terms[0][None, :, None] + x_terms[0][None, None, :]
    anchor = squared == 0.0
    safe_squared = jnp.where(anchor, 1.0, squared)
    damped = jnp.exp(squared * (-(math.pi * math.pi) / (EWALD_SPLIT * EWALD_SPLIT))) / (
        safe_squared * (math.pi * (length * NY * NX))
    )
    fixes = z_terms[1][:, None, None] * y_terms[1][None, :, None] * x_terms[1][None, None, :]
    return jnp.where(anchor, 0.0, damped) * fixes


def tables(length):
    steps = np.arange(length)
    angles = (steps[:, None] * steps[None, :] % length) * (FULL_TURN / length)
    return np.cos(angles).astype(np.float32), np.sin(angles).astype(np.float32)


def transform_by_steps(grid, rows):
    pencils = lax.axis_size("pencil")
    tiles, _, _, _ = grid.shape
    cosine, sine = tables(NX)
    both = np.stack([cosine, -sine], axis=1).reshape(tiles, LANES, 2, NX)
    after_x = jnp.einsum("tzrl,tlck->czrk", grid, both, precision=HIGH)
    got = lax.all_to_all(after_x[:, None], "pencil", split_axis=4, concat_axis=1, tiled=True)
    rim = jnp.roll(got[:, :, :, :RIM], -1, axis=1)
    body = got[:, :, :, RIM:]
    body = jnp.concatenate([body[:, :, :, : rows - RIM], body[:, :, :, rows - RIM :] + rim], axis=3)
    cosine, sine = tables(NY)
    shape = (pencils, rows, NY)
    turn = np.stack([np.stack([cosine, sine]), np.stack([-sine, cosine])])
    turn = turn.reshape(2, 2, *shape)
    after_y = jnp.einsum("dcprk,cpzrx->dzkx", turn, body, precision=HIGH)
    got = lax.all_to_all(after_y, "brick", split_axis=2, concat_axis=1, tiled=True)
    length = got.shape[1]
    cosine, sine = tables(length)
    turn = np.stack([np.stack([cosine, sine]), np.stack([-sine, cosine])])
    transformed = jnp.einsum("dczk,czyx->dkyx", turn, got, precision=HIGH)
    row_part = transformed.shape[2]
    column_part = transformed.shape[3]
    wave_depth = jnp.arange(length, dtype=jnp.int32)
    wave_rows = lax.axis_index("brick") * row_part + jnp.arange(row_part, dtype=jnp.int32)
    wave_columns = lax.axis_index("pencil") * column_part + jnp.arange(column_part, dtype=jnp.int32)
    kernel = ewald_kernel(
        terms_of(wave_depth, length), terms_of(wave_rows, NY), terms_of(wave_columns, NX), length
    )
    power = transformed[0] * transformed[0] + transformed[1] * transformed[1]
    total = lax.psum(jnp.sum(kernel * power), ("brick", "pencil"))
    return total.reshape(1), transformed


def shards(positions, charges, anchor_row, anchor_column, counts):
    slot_count = anchor_row.shape[0]
    atoms = charges.shape[0]
    block_atoms = atoms // slot_count
    rows = NY // lax.axis_size("pencil")
    live = jnp.arange(atoms, dtype=jnp.int32) < counts[0] * block_atoms
    charge = (charges * live.astype(jnp.float32)).reshape(1, atoms)
    other = [
        from_behind(array, "brick", -1) for array in (anchor_row, anchor_column, positions, charge)
    ]
    grid = spread(3, rows, anchor_row, anchor_column, positions, charge)
    grid = spread(0, rows, *other, grid)
    total, spectrum = transform_by_steps(grid, rows)
    slot_total = slot_count * lax.axis_size("brick") * lax.axis_size("pencil")
    return (total * (0.5 / slot_total), spectrum)


def solution(mesh):
    return jax.shard_map(
        shards,
        mesh=mesh,
        in_specs=(
            P(None, ("brick", "pencil")),
            P(("brick", "pencil")),
            P(("brick", "pencil")),
            P(("brick", "pencil")),
            P(("brick", "pencil")),
        ),
        out_specs=(P(), P(None, None, "brick", "pencil")),
        check_vma=False,
    )
```

```python
import functools
import math

import jax
import jax.numpy as jnp
import numpy as np
from jax import lax
from jax.experimental import pallas as pl
from jax.experimental.pallas import tpu as pltpu
from jax.sharding import PartitionSpec as P

NX = 512
NY = 512
ZDEV = 3
PY = 16
PX = 16
LANES = 128
RIM = 8
GROUP = 4

FULL_TURN = 2.0 * math.pi
EWALD_SPLIT = 0.35
HIGH = lax.Precision.HIGH


def from_behind(block, axis, distance):
    devices = range(lax.axis_size(axis))
    route = [((i - distance) % len(devices), i) for i in devices]
    return lax.ppermute(block, axis, route)


def spline(offset):
    distance = jnp.abs(offset - 2.0)
    outer = jnp.maximum(2.0 - distance, 0.0)
    inner = jnp.maximum(1.0 - distance, 0.0)
    return (outer * outer * outer - 4.0 * (inner * inner * inner)) * (1.0 / 6.0)


def split(value):
    high = value.astype(jnp.bfloat16)
    low = (value - high.astype(jnp.float32)).astype(jnp.bfloat16)
    return high, low


def dot3(left, right, dims):
    def one(a, b):
        return lax.dot_general(a, b, (dims, ((), ())), preferred_element_type=jnp.float32)

    return one(left[0], right[1]) + one(left[1], right[0]) + one(left[0], right[0])


def spread_kernel(first_plane, block_atoms, *refs):
    row_ref, column_ref, coords_ref, charge_ref, *before, grid_ref = refs
    slots = row_ref.shape[0]
    if before:
        grid_ref[...] = before[0][...]
    else:
        grid_ref[...] = jnp.zeros_like(grid_ref)
    tiles = grid_ref.shape[0]
    width = GROUP * block_atoms
    lane_block = lax.broadcasted_iota(jnp.int32, (PY, width), 1) // block_atoms
    steps = lax.broadcasted_iota(jnp.int32, (PY, width), 0).astype(jnp.float32)
    planes = (lax.broadcasted_iota(jnp.int32, (8, width), 0) + first_plane).astype(jnp.float32)
    lane = lax.broadcasted_iota(jnp.int32, (ZDEV * PY, LANES), 1)
    blank = jnp.zeros((LANES - PX, width), jnp.bfloat16)

    def turn(step, carry):
        here = pl.ds(pl.multiple_of(step * width, width), width)
        depth = spline(coords_ref[0:1, here] - planes) * charge_ref[0:1, here]
        lines = spline(coords_ref[1:2, here] - steps)
        cells = split(spline(coords_ref[2:3, here] - steps))
        cells = [jnp.concatenate([part, blank], axis=0) for part in cells]
        pieces = []
        for member in range(GROUP):
            own = jnp.where(lane_block == member, lines, 0.0)
            for plane in range(ZDEV):
                pieces.append(split(own * depth[plane : plane + 1]))
        sheets = [jnp.concatenate([piece[i] for piece in pieces], axis=0) for i in range(2)]
        values = dot3(sheets, cells, ((1,), (1,)))
        for member in range(GROUP):
            block = step * GROUP + member
            column = column_ref[block]
            row = row_ref[block] + (RIM - 3)
            shift = column & (LANES - 1)
            tile = column // LANES
            over = (tile + 1) & (tiles - 1)
            patch = values[member * ZDEV * PY : (member + 1) * ZDEV * PY]
            patch = pltpu.roll(patch, shift, 1)
            parts = (
                (tile, jnp.where(lane >= shift, patch, 0.0)),
                (over, jnp.where(lane >= shift, 0.0, patch)),
            )
            sums = []
            for where, part in parts:
                for plane in range(ZDEV):
                    old = grid_ref[where, plane, pl.ds(row, PY), :]
                    sums.append(old + part[plane * PY : (plane + 1) * PY])
            for index, (where, part) in enumerate(parts):
                for plane in range(ZDEV):
                    grid_ref[where, plane, pl.ds(row, PY), :] = sums[index * ZDEV + plane]
        return carry

    lax.fori_loop(0, slots // GROUP, turn, 0)


def spread(first_plane, rows, anchor_row, anchor_column, coords, charge, *before):
    slots = anchor_row.shape[0]
    shape = (NX // LANES, ZDEV, rows + RIM, LANES)
    scalar = pl.BlockSpec(memory_space=pltpu.SMEM)
    whole = pl.BlockSpec(memory_space=pltpu.VMEM)
    return pl.pallas_call(
        functools.partial(spread_kernel, first_plane, charge.shape[1] // slots),
        out_shape=jax.ShapeDtypeStruct(shape, jnp.float32),
        in_specs=[scalar, scalar] + [whole] * (2 + len(before)),
        out_specs=whole,
        compiler_params=pltpu.CompilerParams(vmem_limit_bytes=24 * 1024 * 1024),
        cost_estimate=pl.CostEstimate(
            flops=20_000_000, bytes_accessed=4_000_000, transcendentals=0
        ),
    )(anchor_row, anchor_column, coords, charge, *before)


def terms_of(wave_index, length):
    signed = jnp.where(2 * wave_index >= length, wave_index - length, wave_index)
    fraction = signed.astype(jnp.float32) / length
    cosine = jnp.cos(wave_index.astype(jnp.float32) * (FULL_TURN / length))
    spline_fix = 9.0 / ((2.0 + cosine) * (2.0 + cosine))
    return (fraction * fraction, spline_fix)


def ewald_kernel(z_terms, y_terms, x_terms, length):
    squared = z_terms[0][:, None, None] + y_terms[0][None, :, None] + x_terms[0][None, None, :]
    anchor = squared == 0.0
    safe_squared = jnp.where(anchor, 1.0, squared)
    damped = jnp.exp(squared * (-(math.pi * math.pi) / (EWALD_SPLIT * EWALD_SPLIT))) / (
        safe_squared * (math.pi * (length * NY * NX))
    )
    fixes = z_terms[1][:, None, None] * y_terms[1][None, :, None] * x_terms[1][None, None, :]
    return jnp.where(anchor, 0.0, damped) * fixes


def tables(length):
    steps = np.arange(length)
    angles = (steps[:, None] * steps[None, :] % length) * (FULL_TURN / length)
    return np.cos(angles).astype(np.float32), np.sin(angles).astype(np.float32)


def transform_by_steps(grid, rows):
    pencils = lax.axis_size("pencil")
    tiles, _, _, _ = grid.shape
    cosine, sine = tables(NX)
    both = np.stack([cosine, -sine], axis=1).reshape(tiles, LANES, 2, NX)
    after_x = jnp.einsum("tzrl,tlck->czrk", grid, both, precision=HIGH)
    got = lax.all_to_all(after_x[:, None], "pencil", split_axis=4, concat_axis=1, tiled=True)
    rim = jnp.roll(got[:, :, :, :RIM], -1, axis=1)
    body = got[:, :, :, RIM:]
    body = jnp.concatenate([body[:, :, :, : rows - RIM], body[:, :, :, rows - RIM :] + rim], axis=3)
    cosine, sine = tables(NY)
    shape = (pencils, rows, NY)
    turn = np.stack([np.stack([cosine, sine]), np.stack([-sine, cosine])])
    turn = turn.reshape(2, 2, *shape)
    after_y = jnp.einsum("dcprk,cpzrx->dzkx", turn, body, precision=HIGH)
    got = lax.all_to_all(after_y, "brick", split_axis=2, concat_axis=1, tiled=True)
    length = got.shape[1]
    cosine, sine = tables(length)
    turn = np.stack([np.stack([cosine, sine]), np.stack([-sine, cosine])])
    transformed = jnp.einsum("dczk,czyx->dkyx", turn, got, precision=HIGH)
    row_part = transformed.shape[2]
    column_part = transformed.shape[3]
    wave_depth = jnp.arange(length, dtype=jnp.int32)
    wave_rows = lax.axis_index("brick") * row_part + jnp.arange(row_part, dtype=jnp.int32)
    wave_columns = lax.axis_index("pencil") * column_part + jnp.arange(column_part, dtype=jnp.int32)
    kernel = ewald_kernel(
        terms_of(wave_depth, length), terms_of(wave_rows, NY), terms_of(wave_columns, NX), length
    )
    power = transformed[0] * transformed[0] + transformed[1] * transformed[1]
    total = lax.psum(jnp.sum(kernel * power), ("brick", "pencil"))
    return total.reshape(1), transformed


def wave_terms(length):
    wave = np.arange(length)
    fraction = np.where(2 * wave >= length, wave - length, wave) / length
    fix = 9.0 / (2.0 + np.cos(wave * (FULL_TURN / length))) ** 2
    weight = fix * np.exp(-(math.pi**2) / EWALD_SPLIT**2 * fraction**2)
    return (fraction**2).astype(np.float32), weight.astype(np.float32)


def by_factor(value, angle):
    cosine, sine = math.cos(angle), math.sin(angle)
    real, imag = value
    if abs(sine) < 1e-12 and cosine > 0.0:
        return value
    if abs(cosine) < 1e-12 and sine > 0.0:
        return imag, -real
    return real * cosine + imag * sine, imag * cosine - real * sine


def radix_two(values):
    count = len(values)
    if count == 1:
        return values
    even, odd = radix_two(values[0::2]), radix_two(values[1::2])
    odd = [by_factor(value, FULL_TURN * k / count) for k, value in enumerate(odd)]
    first = [(a[0] + b[0], a[1] + b[1]) for a, b in zip(even, odd)]
    return first + [(a[0] - b[0], a[1] - b[1]) for a, b in zip(even, odd)]


def leading_transform(planes):
    bricks = len(planes[0])
    length = ZDEV * bricks
    parts = [radix_two(plane) for plane in planes]
    result = [None] * length
    for k in range(bricks):
        base = parts[0][k]
        one = by_factor(parts[1][k], FULL_TURN * k / length)
        two = by_factor(parts[2][k], FULL_TURN * 2 * k / length)
        total = (one[0] + two[0], one[1] + two[1])
        apart = ((one[0] - two[0]) * (0.5 * math.sqrt(3.0)), (one[1] - two[1]) * (0.5 * math.sqrt(3.0)))
        middle = (base[0] - 0.5 * total[0], base[1] - 0.5 * total[1])
        result[k] = (base[0] + total[0], base[1] + total[1])
        result[k + bricks] = (middle[0] + apart[1], middle[1] - apart[0])
        result[k + 2 * bricks] = (middle[0] - apart[1], middle[1] + apart[0])
    return result


def fused_kernel(
    pencils, bricks,
    grid_ref, xhigh_ref, xlow_ref, yhigh_ref, ylow_ref, yterm_ref, xterm_ref,
    energy_ref, spectrum_ref,
    xs, xr, ys, zr, ep, eb,
    xsend, xrecv, zsend, zrecv, epsend, eprecv, ebsend, ebrecv,
):
    mine = {"pencil": lax.axis_index("pencil"), "brick": lax.axis_index("brick")}
    sizes = {"pencil": pencils, "brick": bricks}
    part = NY // bricks
    rows = NY // pencils
    started = []

    def peer(axis, step):
        return lax.rem(mine[axis] + step, sizes[axis])

    def send(axis, step, source, target, send_sem, recv_sem):
        copy = pltpu.make_async_remote_copy(
            src_ref=source, dst_ref=target, send_sem=send_sem, recv_sem=recv_sem,
            device_id={axis: peer(axis, step)}, device_id_type=pl.DeviceIdType.MESH,
        )
        copy.start()
        started.append(copy)

    def arrived(axis, step, target, recv_sem, send_sem):
        pltpu.make_async_remote_copy(
            src_ref=target, dst_ref=target, send_sem=send_sem, recv_sem=recv_sem,
            device_id={axis: peer(axis, step)}, device_id_type=pl.DeviceIdType.MESH,
        ).wait_recv()

    barrier = pltpu.get_barrier_semaphore()
    for axis in sizes:
        for step in range(1, sizes[axis]):
            pl.semaphore_signal(
                barrier, inc=1, device_id={axis: peer(axis, step)},
                device_id_type=pl.DeviceIdType.MESH,
            )

    me, slab = mine["pencil"], mine["brick"]
    for plane in range(ZDEV):
        lines = jnp.concatenate([grid_ref[t, plane] for t in range(NX // LANES)], axis=1)
        after_x = dot3(split(lines), (xhigh_ref[...], xlow_ref[...]), ((1,), (0,)))
        width = after_x.shape[1] // pencils
        for target in range(pencils):
            xs[plane, target] = after_x[:, target * width : (target + 1) * width]
        if plane == 0:
            pl.semaphore_wait(barrier, pencils + bricks - 2)
        for step in range(1, pencils):
            send(
                "pencil", step, xs.at[plane, peer("pencil", step)], xr.at[plane, me],
                xsend.at[plane, step], xrecv.at[plane, me],
            )
        xr[plane, me] = xs[plane, me]

    for plane in range(ZDEV):
        for step in range(1, pencils):
            other = peer("pencil", step)
            arrived("pencil", step, xr.at[plane, other], xrecv.at[plane, other], xsend.at[plane, step])
        pieces = []
        for source in range(pencils):
            pieces.append(xr[plane, source, RIM:rows])
            rim = xr[plane, (source + 1) % pencils, 0:RIM]
            pieces.append(xr[plane, source, rows : rows + RIM] + rim)
        columns = split(jnp.concatenate(pieces, axis=0))
        both = dot3((yhigh_ref[...], ylow_ref[...]), columns, ((1,), (0,)))
        real = both[:NY, :LANES] + both[NY:, LANES:]
        imag = both[:NY, LANES:] - both[NY:, :LANES]
        for target in range(bricks):
            ys[plane, target, :, 0:LANES] = real[target * part : (target + 1) * part]
            ys[plane, target, :, LANES:] = imag[target * part : (target + 1) * part]
        for step in range(1, bricks):
            send(
                "brick", step, ys.at[plane, peer("brick", step)], zr.at[plane, slab],
                zsend.at[plane, step], zrecv.at[plane, slab],
            )
        zr[plane, slab] = ys[plane, slab]

    for plane in range(ZDEV):
        for step in range(1, bricks):
            other = peer("brick", step)
            arrived("brick", step, zr.at[plane, other], zrecv.at[plane, other], zsend.at[plane, step])

    length = ZDEV * bricks
    depth_square, depth_weight = wave_terms(length)
    lanes = pl.ds(pl.multiple_of(me * LANES, LANES), LANES)

    def chunk(step, total):
        here = pl.ds(pl.multiple_of(step * 8, 8), 8)
        planes = [
            [(zr[i, b, here, 0:LANES], zr[i, b, here, LANES : 2 * LANES]) for b in range(bricks)]
            for i in range(ZDEV)
        ]
        result = leading_transform(planes)
        across = pl.ds(pl.multiple_of(slab * part + step * 8, 8), 8)
        square = yterm_ref[0, across, :] + xterm_ref[0, :, lanes]
        weight = yterm_ref[1, across, :] * xterm_ref[1, :, lanes]
        powers = {}
        for k, (real, imag) in enumerate(result):
            spectrum_ref[0, k, here, :] = real
            spectrum_ref[1, k, here, :] = imag
            fold = min(k, length - k)
            powers[fold] = powers.get(fold, 0.0) + (real * real + imag * imag)
        inner = jnp.zeros_like(total)
        for k, power in powers.items():
            q = square + float(depth_square[k])
            term = float(depth_weight[k]) * power / jnp.where(q == 0.0, 1.0, q)
            inner = inner + (jnp.where(q == 0.0, 0.0, term) if k == 0 else term)
        return total + inner * weight

    share = lax.fori_loop(0, part // 8, chunk, jnp.zeros((8, LANES), jnp.float32))
    share = share * (1.0 / (math.pi * (length * NY * NX)))
    for axis, held, sends, recvs in (
        ("pencil", ep, epsend, eprecv), ("brick", eb, ebsend, ebrecv),
    ):
        own = mine[axis]
        held[own] = share
        for step in range(1, sizes[axis]):
            send(axis, step, held.at[own], held.at[own], sends.at[step], recvs.at[own])
        for step in range(1, sizes[axis]):
            other = peer(axis, step)
            arrived(axis, step, held.at[other], recvs.at[other], sends.at[step])
        share = held[0]
        for source in range(1, sizes[axis]):
            share = share + held[source]
    energy_ref[...] = share
    for copy in started:
        copy.wait_send()


def transform_fused(grid, rows):
    pencils, bricks = lax.axis_size("pencil"), lax.axis_size("brick")
    part = NY // bricks
    columns = NX // pencils
    cosine, sine = tables(NX)
    turn_x = np.stack(
        [cosine.reshape(NX, pencils, columns), -sine.reshape(NX, pencils, columns)], axis=2
    ).reshape(NX, 2 * NX)
    cosine, sine = tables(NY)
    turn_y = np.concatenate([cosine, sine], axis=0)

    def halves(table):
        high = table.astype(jnp.bfloat16)
        return high, (table - high.astype(np.float32)).astype(jnp.bfloat16)

    y_terms = np.broadcast_to(np.stack(wave_terms(NY))[:, :, None], (2, NY, LANES))
    x_terms = np.broadcast_to(np.stack(wave_terms(NX))[:, None, :], (2, 8, NX))
    f32 = jnp.float32
    whole = pl.BlockSpec(memory_space=pltpu.VMEM)
    dma = pltpu.SemaphoreType.DMA
    energy, spectrum = pl.pallas_call(
        functools.partial(fused_kernel, pencils, bricks),
        out_shape=(
            jax.ShapeDtypeStruct((8, LANES), f32),
            jax.ShapeDtypeStruct((2, ZDEV * bricks, part, columns), f32),
        ),
        in_specs=[whole] * 7,
        out_specs=(whole, whole),
        scratch_shapes=[
            pltpu.VMEM((ZDEV, pencils, rows + RIM, 2 * LANES), f32),
            pltpu.VMEM((ZDEV, pencils, rows + RIM, 2 * LANES), f32),
            pltpu.VMEM((ZDEV, bricks, part, 2 * LANES), f32),
            pltpu.VMEM((ZDEV, bricks, part, 2 * LANES), f32),
            pltpu.VMEM((pencils, 8, LANES), f32),
            pltpu.VMEM((bricks, 8, LANES), f32),
            dma((ZDEV, pencils)), dma((ZDEV, pencils)),
            dma((ZDEV, bricks)), dma((ZDEV, bricks)),
            dma((pencils,)), dma((pencils,)), dma((bricks,)), dma((bricks,)),
        ],
        compiler_params=pltpu.CompilerParams(
            collective_id=0, has_side_effects=True, vmem_limit_bytes=40 * 1024 * 1024
        ),
        cost_estimate=pl.CostEstimate(
            flops=6_000_000_000, bytes_accessed=8_000_000, transcendentals=0
        ),
    )(grid, *halves(turn_x), *halves(turn_y), y_terms.astype(np.float32), x_terms.astype(np.float32))
    return jnp.sum(energy).reshape(1), spectrum


def shards(positions, charges, anchor_row, anchor_column, counts):
    slot_count = anchor_row.shape[0]
    atoms = charges.shape[0]
    block_atoms = atoms // slot_count
    rows = NY // lax.axis_size("pencil")
    live = jnp.arange(atoms, dtype=jnp.int32) < counts[0] * block_atoms
    charge = (charges * live.astype(jnp.float32)).reshape(1, atoms)
    other = [
        from_behind(array, "brick", -1) for array in (anchor_row, anchor_column, positions, charge)
    ]
    grid = spread(3, rows, anchor_row, anchor_column, positions, charge)
    grid = spread(0, rows, *other, grid)
    bricks = lax.axis_size("brick")
    tiled = NX // lax.axis_size("pencil") == LANES and NY // bricks % 8 == 0
    if tiled and bricks & (bricks - 1) == 0:
        total, spectrum = transform_fused(grid, rows)
    else:
        total, spectrum = transform_by_steps(grid, rows)
    slot_total = slot_count * lax.axis_size("brick") * lax.axis_size("pencil")
    return (total * (0.5 / slot_total), spectrum)


def solution(mesh):
    return jax.shard_map(
        shards,
        mesh=mesh,
        in_specs=(
            P(None, ("brick", "pencil")),
            P(("brick", "pencil")),
            P(("brick", "pencil")),
            P(("brick", "pencil")),
            P(("brick", "pencil")),
        ),
        out_specs=(P(), P(None, None, "brick", "pencil")),
        check_vma=False,
    )
```

```python
import functools
import math

import jax
import jax.numpy as jnp
import numpy as np
from jax import lax
from jax.experimental import pallas as pl
from jax.experimental.pallas import tpu as pltpu
from jax.sharding import PartitionSpec as P

NX = 512
NY = 512
ZDEV = 3
PY = 16
PX = 16
LANES = 128
RIM = 8
GROUP = 4

FULL_TURN = 2.0 * math.pi
EWALD_SPLIT = 0.35
HIGH = lax.Precision.HIGH


def from_behind(block, axis, distance):
    devices = range(lax.axis_size(axis))
    route = [((i - distance) % len(devices), i) for i in devices]
    return lax.ppermute(block, axis, route)


def spline(offset):
    distance = jnp.abs(offset - 2.0)
    outer = jnp.maximum(2.0 - distance, 0.0)
    inner = jnp.maximum(1.0 - distance, 0.0)
    return (outer * outer * outer - 4.0 * (inner * inner * inner)) * (1.0 / 6.0)


def split(value):
    high = value.astype(jnp.bfloat16)
    low = (value - high.astype(jnp.float32)).astype(jnp.bfloat16)
    return high, low


def dot3(left, right, dims):
    def one(a, b):
        return lax.dot_general(a, b, (dims, ((), ())), preferred_element_type=jnp.float32)

    return one(left[0], right[1]) + one(left[1], right[0]) + one(left[0], right[0])


def spread_kernel(first_plane, block_atoms, *refs):
    anchor_ref, coords_ref, *before, grid_ref = refs
    slots = anchor_ref.shape[0] // 2
    if before:
        grid_ref[...] = before[0][...]
    else:
        grid_ref[...] = jnp.zeros_like(grid_ref)
    tiles = grid_ref.shape[0]
    width = GROUP * block_atoms
    lane_block = lax.broadcasted_iota(jnp.int32, (PY, width), 1) // block_atoms
    steps = lax.broadcasted_iota(jnp.int32, (PY, width), 0).astype(jnp.float32)
    planes = (lax.broadcasted_iota(jnp.int32, (8, width), 0) + first_plane).astype(jnp.float32)
    lane = lax.broadcasted_iota(jnp.int32, (ZDEV * PY, LANES), 1)
    blank = jnp.zeros((LANES - PX, width), jnp.bfloat16)

    def turn(step, carry):
        here = pl.ds(pl.multiple_of(step * width, width), width)
        depth = spline(coords_ref[0:1, here] - planes) * coords_ref[3:4, here]
        lines = spline(coords_ref[1:2, here] - steps)
        cells = split(spline(coords_ref[2:3, here] - steps))
        cells = [jnp.concatenate([part, blank], axis=0) for part in cells]
        pieces = []
        for member in range(GROUP):
            own = jnp.where(lane_block == member, lines, 0.0)
            for plane in range(ZDEV):
                pieces.append(split(own * depth[plane : plane + 1]))
        sheets = [jnp.concatenate([piece[i] for piece in pieces], axis=0) for i in range(2)]
        values = dot3(sheets, cells, ((1,), (1,)))
        for member in range(GROUP):
            block = step * GROUP + member
            column = anchor_ref[slots + block]
            row = anchor_ref[block] + (RIM - 3)
            shift = column & (LANES - 1)
            tile = column // LANES
            over = (tile + 1) & (tiles - 1)
            patch = values[member * ZDEV * PY : (member + 1) * ZDEV * PY]
            patch = pltpu.roll(patch, shift, 1)
            parts = (
                (tile, jnp.where(lane >= shift, patch, 0.0)),
                (over, jnp.where(lane >= shift, 0.0, patch)),
            )
            sums = []
            for where, part in parts:
                for plane in range(ZDEV):
                    old = grid_ref[where, plane, pl.ds(row, PY), :]
                    sums.append(old + part[plane * PY : (plane + 1) * PY])
            for index, (where, part) in enumerate(parts):
                for plane in range(ZDEV):
                    grid_ref[where, plane, pl.ds(row, PY), :] = sums[index * ZDEV + plane]
        return carry

    lax.fori_loop(0, slots // GROUP, turn, 0, unroll=4)


def spread(first_plane, rows, anchors, coords, *before):
    slots = anchors.shape[0] // 2
    shape = (NX // LANES, ZDEV, rows + RIM, LANES)
    scalar = pl.BlockSpec(memory_space=pltpu.SMEM)
    whole = pl.BlockSpec(memory_space=pltpu.VMEM)
    return pl.pallas_call(
        functools.partial(spread_kernel, first_plane, coords.shape[1] // slots),
        out_shape=jax.ShapeDtypeStruct(shape, jnp.float32),
        in_specs=[scalar] + [whole] * (1 + len(before)),
        out_specs=whole,
        compiler_params=pltpu.CompilerParams(vmem_limit_bytes=10 * 1024 * 1024),
        cost_estimate=pl.CostEstimate(
            flops=20_000_000, bytes_accessed=4_000_000, transcendentals=0
        ),
    )(anchors, coords, *before)


def terms_of(wave_index, length):
    signed = jnp.where(2 * wave_index >= length, wave_index - length, wave_index)
    fraction = signed.astype(jnp.float32) / length
    cosine = jnp.cos(wave_index.astype(jnp.float32) * (FULL_TURN / length))
    spline_fix = 9.0 / ((2.0 + cosine) * (2.0 + cosine))
    return (fraction * fraction, spline_fix)


def ewald_kernel(z_terms, y_terms, x_terms, length):
    squared = z_terms[0][:, None, None] + y_terms[0][None, :, None] + x_terms[0][None, None, :]
    anchor = squared == 0.0
    safe_squared = jnp.where(anchor, 1.0, squared)
    damped = jnp.exp(squared * (-(math.pi * math.pi) / (EWALD_SPLIT * EWALD_SPLIT))) / (
        safe_squared * (math.pi * (length * NY * NX))
    )
    fixes = z_terms[1][:, None, None] * y_terms[1][None, :, None] * x_terms[1][None, None, :]
    return jnp.where(anchor, 0.0, damped) * fixes


def tables(length):
    steps = np.arange(length)
    angles = (steps[:, None] * steps[None, :] % length) * (FULL_TURN / length)
    return np.cos(angles).astype(np.float32), np.sin(angles).astype(np.float32)


def transform_by_steps(grid, rows):
    pencils = lax.axis_size("pencil")
    tiles, _, _, _ = grid.shape
    cosine, sine = tables(NX)
    both = np.stack([cosine, -sine], axis=1).reshape(tiles, LANES, 2, NX)
    after_x = jnp.einsum("tzrl,tlck->czrk", grid, both, precision=HIGH)
    got = lax.all_to_all(after_x[:, None], "pencil", split_axis=4, concat_axis=1, tiled=True)
    rim = jnp.roll(got[:, :, :, :RIM], -1, axis=1)
    body = got[:, :, :, RIM:]
    body = jnp.concatenate([body[:, :, :, : rows - RIM], body[:, :, :, rows - RIM :] + rim], axis=3)
    cosine, sine = tables(NY)
    shape = (pencils, rows, NY)
    turn = np.stack([np.stack([cosine, sine]), np.stack([-sine, cosine])])
    turn = turn.reshape(2, 2, *shape)
    after_y = jnp.einsum("dcprk,cpzrx->dzkx", turn, body, precision=HIGH)
    got = lax.all_to_all(after_y, "brick", split_axis=2, concat_axis=1, tiled=True)
    length = got.shape[1]
    cosine, sine = tables(length)
    turn = np.stack([np.stack([cosine, sine]), np.stack([-sine, cosine])])
    transformed = jnp.einsum("dczk,czyx->dkyx", turn, got, precision=HIGH)
    row_part = transformed.shape[2]
    column_part = transformed.shape[3]
    wave_depth = jnp.arange(length, dtype=jnp.int32)
    wave_rows = lax.axis_index("brick") * row_part + jnp.arange(row_part, dtype=jnp.int32)
    wave_columns = lax.axis_index("pencil") * column_part + jnp.arange(column_part, dtype=jnp.int32)
    kernel = ewald_kernel(
        terms_of(wave_depth, length), terms_of(wave_rows, NY), terms_of(wave_columns, NX), length
    )
    power = transformed[0] * transformed[0] + transformed[1] * transformed[1]
    total = lax.psum(jnp.sum(kernel * power), ("brick", "pencil"))
    return total.reshape(1), transformed


def wave_terms(length):
    wave = np.arange(length)
    fraction = np.where(2 * wave >= length, wave - length, wave) / length
    fix = 9.0 / (2.0 + np.cos(wave * (FULL_TURN / length))) ** 2
    weight = fix * np.exp(-(math.pi**2) / EWALD_SPLIT**2 * fraction**2)
    return (fraction**2).astype(np.float32), weight.astype(np.float32)


def by_factor(value, angle):
    cosine, sine = math.cos(angle), math.sin(angle)
    real, imag = value
    if abs(sine) < 1e-12 and cosine > 0.0:
        return value
    if abs(cosine) < 1e-12 and sine > 0.0:
        return imag, -real
    return real * cosine + imag * sine, imag * cosine - real * sine


def radix_two(values):
    count = len(values)
    if count == 1:
        return values
    even, odd = radix_two(values[0::2]), radix_two(values[1::2])
    odd = [by_factor(value, FULL_TURN * k / count) for k, value in enumerate(odd)]
    first = [(a[0] + b[0], a[1] + b[1]) for a, b in zip(even, odd)]
    return first + [(a[0] - b[0], a[1] - b[1]) for a, b in zip(even, odd)]


def leading_transform(parts):
    bricks = len(parts[0])
    length = ZDEV * bricks
    result = [None] * length
    for k in range(bricks):
        base = parts[0][k]
        one = by_factor(parts[1][k], FULL_TURN * k / length)
        two = by_factor(parts[2][k], FULL_TURN * 2 * k / length)
        total = (one[0] + two[0], one[1] + two[1])
        apart = ((one[0] - two[0]) * (0.5 * math.sqrt(3.0)), (one[1] - two[1]) * (0.5 * math.sqrt(3.0)))
        middle = (base[0] - 0.5 * total[0], base[1] - 0.5 * total[1])
        result[k] = (base[0] + total[0], base[1] + total[1])
        result[k + bricks] = (middle[0] + apart[1], middle[1] - apart[0])
        result[k + 2 * bricks] = (middle[0] - apart[1], middle[1] + apart[0])
    return result


def fused_kernel(
    pencils, bricks,
    grid_ref, xhigh_ref, xlow_ref, yhigh_any, ylow_any, yterm_any, xterm_ref,
    energy_ref, spectrum_ref,
    yhigh_ref, ylow_ref, yterm_ref, fetched, xs, xr, ys, zr, ep, eb,
    xsend, xrecv, zsend, zrecv, epsend, eprecv, ebsend, ebrecv,
):
    mine = {"pencil": lax.axis_index("pencil"), "brick": lax.axis_index("brick")}
    sizes = {"pencil": pencils, "brick": bricks}
    part = NY // bricks
    rows = NY // pencils
    started = []

    def peer(axis, step):
        half = sizes[axis] // 2
        side, place = mine[axis] // half, mine[axis] % half
        if step <= half:
            return (1 - side) * half + lax.rem(place + step - 1, half)
        return side * half + lax.rem(place + step - half, half)

    def send(axis, step, source, target, send_sem, recv_sem):
        copy = pltpu.make_async_remote_copy(
            src_ref=source, dst_ref=target, send_sem=send_sem, recv_sem=recv_sem,
            device_id={axis: peer(axis, step)}, device_id_type=pl.DeviceIdType.MESH,
        )
        copy.start()
        started.append(copy)

    def arrived(axis, step, target, recv_sem, send_sem):
        pltpu.make_async_remote_copy(
            src_ref=target, dst_ref=target, send_sem=send_sem, recv_sem=recv_sem,
            device_id={axis: peer(axis, step)}, device_id_type=pl.DeviceIdType.MESH,
        ).wait_recv()

    fetches = [
        pltpu.make_async_copy(source, target, fetched.at[i])
        for i, (source, target) in enumerate(
            [(yhigh_any, yhigh_ref), (ylow_any, ylow_ref), (yterm_any, yterm_ref)]
        )
    ]
    for fetch in fetches:
        fetch.start()
    barrier = pltpu.get_barrier_semaphore()
    for axis in sizes:
        for step in range(1, sizes[axis]):
            pl.semaphore_signal(
                barrier, inc=1, device_id={axis: peer(axis, step)},
                device_id_type=pl.DeviceIdType.MESH,
            )

    me, slab = mine["pencil"], mine["brick"]

    def send_lines(plane):
        for step in range(1, pencils):
            send(
                "pencil", step, xs.at[plane, peer("pencil", step)], xr.at[plane, me],
                xsend.at[plane, step], xrecv.at[plane, me],
            )

    for plane in range(ZDEV):
        lines = jnp.concatenate([grid_ref[t, plane] for t in range(NX // LANES)], axis=1)
        after_x = dot3(split(lines), (xhigh_ref[...], xlow_ref[...]), ((1,), (0,)))
        width = after_x.shape[1] // pencils
        for target in range(pencils):
            xs[plane, target] = after_x[:, target * width : (target + 1) * width]
        if plane == 0:
            pl.semaphore_wait(barrier, pencils + bricks - 2)
            send_lines(plane)
        xr[plane, me] = xs[plane, me]

    for plane in range(ZDEV):
        for step in range(1, pencils):
            other = peer("pencil", step)
            arrived("pencil", step, xr.at[plane, other], xrecv.at[plane, other], xsend.at[plane, step])
        if plane + 1 < ZDEV:
            send_lines(plane + 1)
        if plane == 0:
            for fetch in fetches:
                fetch.wait()
        pieces = []
        for source in range(pencils):
            pieces.append(xr[plane, source, RIM:rows])
            rim = xr[plane, (source + 1) % pencils, 0:RIM]
            pieces.append(xr[plane, source, rows : rows + RIM] + rim)
        columns = split(jnp.concatenate(pieces, axis=0))
        both = dot3((yhigh_ref[...], ylow_ref[...]), columns, ((1,), (0,)))
        real = both[:NY, :LANES] + both[NY:, LANES:]
        imag = both[:NY, LANES:] - both[NY:, :LANES]
        for target in range(bricks):
            ys[plane, target, :, 0:LANES] = real[target * part : (target + 1) * part]
            ys[plane, target, :, LANES:] = imag[target * part : (target + 1) * part]
        for step in range(1, bricks):
            send(
                "brick", step, ys.at[plane, peer("brick", step)], zr.at[plane, slab],
                zsend.at[plane, step], zrecv.at[plane, slab],
            )
        zr[plane, slab] = ys[plane, slab]

    def over_bricks(plane, step, carry):
        here = pl.ds(pl.multiple_of(step * 8, 8), 8)
        values = [
            (zr[plane, b, here, 0:LANES], zr[plane, b, here, LANES : 2 * LANES])
            for b in range(bricks)
        ]
        for k, (real, imag) in enumerate(radix_two(values)):
            zr[plane, k, here, 0:LANES] = real
            zr[plane, k, here, LANES : 2 * LANES] = imag
        return carry

    for plane in range(ZDEV):
        for step in range(1, bricks):
            other = peer("brick", step)
            arrived("brick", step, zr.at[plane, other], zrecv.at[plane, other], zsend.at[plane, step])
        if plane + 1 < ZDEV:
            lax.fori_loop(0, part // 8, functools.partial(over_bricks, plane), 0)

    length = ZDEV * bricks
    depth_square, depth_weight = wave_terms(length)
    lanes = pl.ds(pl.multiple_of(me * LANES, LANES), LANES)

    def chunk(step, total):
        here = pl.ds(pl.multiple_of(step * 8, 8), 8)
        planes = [
            [(zr[i, b, here, 0:LANES], zr[i, b, here, LANES : 2 * LANES]) for b in range(bricks)]
            for i in range(ZDEV)
        ]
        result = leading_transform(planes[:-1] + [radix_two(planes[-1])])
        across = pl.ds(pl.multiple_of(slab * part + step * 8, 8), 8)
        square = yterm_ref[0, across, :] + xterm_ref[0, :, lanes]
        weight = yterm_ref[1, across, :] * xterm_ref[1, :, lanes]
        powers = {}
        for k, (real, imag) in enumerate(result):
            spectrum_ref[0, k, here, :] = real
            spectrum_ref[1, k, here, :] = imag
            fold = min(k, length - k)
            powers[fold] = powers.get(fold, 0.0) + (real * real + imag * imag)
        inner = jnp.zeros_like(total)
        for k, power in powers.items():
            q = square + float(depth_square[k])
            term = float(depth_weight[k]) * power / jnp.where(q == 0.0, 1.0, q)
            inner = inner + (jnp.where(q == 0.0, 0.0, term) if k == 0 else term)
        return total + inner * weight

    share = lax.fori_loop(0, part // 8, chunk, jnp.zeros((8, LANES), jnp.float32))
    share = share * (1.0 / (math.pi * (length * NY * NX)))
    for axis, held, sends, recvs in (
        ("pencil", ep, epsend, eprecv), ("brick", eb, ebsend, ebrecv),
    ):
        own = mine[axis]
        held[own] = share
        for step in range(1, sizes[axis]):
            send(axis, step, held.at[own], held.at[own], sends.at[step], recvs.at[own])
        for step in range(1, sizes[axis]):
            other = peer(axis, step)
            arrived(axis, step, held.at[other], recvs.at[other], sends.at[step])
        share = held[0]
        for source in range(1, sizes[axis]):
            share = share + held[source]
    energy_ref[...] = share
    for copy in started:
        copy.wait_send()


def transform_fused(grid, rows):
    pencils, bricks = lax.axis_size("pencil"), lax.axis_size("brick")
    part = NY // bricks
    columns = NX // pencils
    cosine, sine = tables(NX)
    turn_x = np.stack(
        [cosine.reshape(NX, pencils, columns), -sine.reshape(NX, pencils, columns)], axis=2
    ).reshape(NX, 2 * NX)
    cosine, sine = tables(NY)
    turn_y = np.concatenate([cosine, sine], axis=0)

    def halves(table):
        high = table.astype(jnp.bfloat16)
        return high, (table - high.astype(np.float32)).astype(jnp.bfloat16)

    y_terms = np.broadcast_to(np.stack(wave_terms(NY))[:, :, None], (2, NY, LANES))
    x_terms = np.broadcast_to(np.stack(wave_terms(NX))[:, None, :], (2, 8, NX))
    f32 = jnp.float32
    whole = pl.BlockSpec(memory_space=pltpu.VMEM)
    dma = pltpu.SemaphoreType.DMA
    energy, spectrum = pl.pallas_call(
        functools.partial(fused_kernel, pencils, bricks),
        out_shape=(
            jax.ShapeDtypeStruct((8, LANES), f32),
            jax.ShapeDtypeStruct((2, ZDEV * bricks, part, columns), f32),
        ),
        in_specs=[whole] * 3 + [pl.BlockSpec(memory_space=pl.ANY)] * 3 + [whole],
        out_specs=(whole, whole),
        scratch_shapes=[
            pltpu.VMEM((2 * NY, NY), jnp.bfloat16),
            pltpu.VMEM((2 * NY, NY), jnp.bfloat16),
            pltpu.VMEM((2, NY, LANES), f32),
            dma((3,)),
            pltpu.VMEM((ZDEV, pencils, rows + RIM, 2 * LANES), f32),
            pltpu.VMEM((ZDEV, pencils, rows + RIM, 2 * LANES), f32),
            pltpu.VMEM((ZDEV, bricks, part, 2 * LANES), f32),
            pltpu.VMEM((ZDEV, bricks, part, 2 * LANES), f32),
            pltpu.VMEM((pencils, 8, LANES), f32),
            pltpu.VMEM((bricks, 8, LANES), f32),
            dma((ZDEV, pencils)), dma((ZDEV, pencils)),
            dma((ZDEV, bricks)), dma((ZDEV, bricks)),
            dma((pencils,)), dma((pencils,)), dma((bricks,)), dma((bricks,)),
        ],
        compiler_params=pltpu.CompilerParams(
            collective_id=0, has_side_effects=True, vmem_limit_bytes=24 * 1024 * 1024
        ),
        cost_estimate=pl.CostEstimate(
            flops=6_000_000_000, bytes_accessed=8_000_000, transcendentals=0
        ),
    )(grid, *halves(turn_x), *halves(turn_y), y_terms.astype(np.float32), x_terms.astype(np.float32))
    return jnp.sum(energy).reshape(1), spectrum


def shards(positions, charges, anchor_row, anchor_column, counts):
    slot_count = anchor_row.shape[0]
    atoms = charges.shape[0]
    block_atoms = atoms // slot_count
    rows = NY // lax.axis_size("pencil")
    live = jnp.arange(atoms, dtype=jnp.int32) < counts[0] * block_atoms
    charge = (charges * live.astype(jnp.float32)).reshape(1, atoms)
    coords = jnp.concatenate([positions, charge], axis=0)
    anchors = jnp.concatenate([anchor_row, anchor_column])
    grid = spread(3, rows, anchors, coords)
    grid, anchors, coords = lax.optimization_barrier((grid, anchors, coords))
    anchors, coords = (from_behind(array, "brick", -1) for array in (anchors, coords))
    grid = spread(0, rows, anchors, coords, grid)
    bricks = lax.axis_size("brick")
    tiled = NX // lax.axis_size("pencil") == LANES and NY // bricks % 8 == 0
    if tiled and bricks & (bricks - 1) == 0:
        total, spectrum = transform_fused(grid, rows)
    else:
        total, spectrum = transform_by_steps(grid, rows)
    slot_total = slot_count * lax.axis_size("brick") * lax.axis_size("pencil")
    return (total * (0.5 / slot_total), spectrum)


def solution(mesh):
    return jax.shard_map(
        shards,
        mesh=mesh,
        in_specs=(
            P(None, ("brick", "pencil")),
            P(("brick", "pencil")),
            P(("brick", "pencil")),
            P(("brick", "pencil")),
            P(("brick", "pencil")),
        ),
        out_specs=(P(), P(None, None, "brick", "pencil")),
        check_vma=False,
    )
```

```python
import functools
import math

import jax
import jax.numpy as jnp
import numpy as np
from jax import lax
from jax.experimental import pallas as pl
from jax.experimental.pallas import tpu as pltpu
from jax.sharding import PartitionSpec as P

NX = 512
NY = 512
ZDEV = 3
PY = 16
PX = 16
LANES = 128
RIM = 8
GROUP = 4

FULL_TURN = 2.0 * math.pi
EWALD_SPLIT = 0.35
HIGH = lax.Precision.HIGH


def from_behind(block, axis, distance):
    devices = range(lax.axis_size(axis))
    route = [((i - distance) % len(devices), i) for i in devices]
    return lax.ppermute(block, axis, route)


def spline(offset):
    distance = jnp.abs(offset - 2.0)
    outer = jnp.maximum(2.0 - distance, 0.0)
    inner = jnp.maximum(1.0 - distance, 0.0)
    return (outer * outer * outer - 4.0 * (inner * inner * inner)) * (1.0 / 6.0)


def split(value):
    high = value.astype(jnp.bfloat16)
    low = (value - high.astype(jnp.float32)).astype(jnp.bfloat16)
    return high, low


def dot3(left, right, dims):
    def one(a, b):
        return lax.dot_general(a, b, (dims, ((), ())), preferred_element_type=jnp.float32)

    return one(left[0], right[1]) + one(left[1], right[0]) + one(left[0], right[0])


def spread_kernel(first_plane, block_atoms, *refs):
    anchor_ref, coords_ref, *before, grid_ref = refs
    slots = anchor_ref.shape[0] // 2
    count = anchor_ref[2 * slots]
    if before:
        grid_ref[...] = before[0][...]
    else:
        grid_ref[...] = jnp.zeros_like(grid_ref)
    tiles = grid_ref.shape[0]
    width = GROUP * block_atoms
    lane_block = lax.broadcasted_iota(jnp.int32, (PY, width), 1) // block_atoms
    steps = lax.broadcasted_iota(jnp.int32, (PY, width), 0).astype(jnp.float32)
    planes = (lax.broadcasted_iota(jnp.int32, (8, width), 0) + first_plane).astype(jnp.float32)
    lane = lax.broadcasted_iota(jnp.int32, (ZDEV * PY, LANES), 1)
    blank = jnp.zeros((LANES - PX, width), jnp.bfloat16)

    def turn(step, carry):
        here = pl.ds(pl.multiple_of(step * width, width), width)
        live = lane_block[0:1] + step * GROUP < count
        charge = jnp.where(live, coords_ref[3:4, here], 0.0)
        depth = spline(coords_ref[0:1, here] - planes) * charge
        lines = spline(coords_ref[1:2, here] - steps)
        cells = split(spline(coords_ref[2:3, here] - steps))
        cells = [jnp.concatenate([part, blank], axis=0) for part in cells]
        pieces = []
        for member in range(GROUP):
            own = jnp.where(lane_block == member, lines, 0.0)
            for plane in range(ZDEV):
                pieces.append(split(own * depth[plane : plane + 1]))
        sheets = [jnp.concatenate([piece[i] for piece in pieces], axis=0) for i in range(2)]
        values = dot3(sheets, cells, ((1,), (1,)))
        for member in range(GROUP):
            block = step * GROUP + member
            column = anchor_ref[slots + block]
            row = anchor_ref[block] + (RIM - 3)
            shift = column & (LANES - 1)
            tile = column // LANES
            over = (tile + 1) & (tiles - 1)
            patch = values[member * ZDEV * PY : (member + 1) * ZDEV * PY]
            patch = pltpu.roll(patch, shift, 1)
            parts = (
                (tile, jnp.where(lane >= shift, patch, 0.0)),
                (over, jnp.where(lane >= shift, 0.0, patch)),
            )
            sums = []
            for where, part in parts:
                for plane in range(ZDEV):
                    old = grid_ref[where, plane, pl.ds(row, PY), :]
                    sums.append(old + part[plane * PY : (plane + 1) * PY])
            for index, (where, part) in enumerate(parts):
                for plane in range(ZDEV):
                    grid_ref[where, plane, pl.ds(row, PY), :] = sums[index * ZDEV + plane]
        return carry

    lax.fori_loop(0, slots // GROUP, turn, 0, unroll=4)


def spread(first_plane, rows, anchors, coords, *before):
    slots = anchors.shape[0] // 2
    shape = (NX // LANES, ZDEV, rows + RIM, LANES)
    scalar = pl.BlockSpec(memory_space=pltpu.SMEM)
    whole = pl.BlockSpec(memory_space=pltpu.VMEM)
    return pl.pallas_call(
        functools.partial(spread_kernel, first_plane, coords.shape[1] // slots),
        out_shape=jax.ShapeDtypeStruct(shape, jnp.float32),
        in_specs=[scalar] + [whole] * (1 + len(before)),
        out_specs=whole,
        compiler_params=pltpu.CompilerParams(vmem_limit_bytes=10 * 1024 * 1024),
        cost_estimate=pl.CostEstimate(
            flops=20_000_000, bytes_accessed=4_000_000, transcendentals=0
        ),
    )(anchors, coords, *before)


def terms_of(wave_index, length):
    signed = jnp.where(2 * wave_index >= length, wave_index - length, wave_index)
    fraction = signed.astype(jnp.float32) / length
    cosine = jnp.cos(wave_index.astype(jnp.float32) * (FULL_TURN / length))
    spline_fix = 9.0 / ((2.0 + cosine) * (2.0 + cosine))
    return (fraction * fraction, spline_fix)


def ewald_kernel(z_terms, y_terms, x_terms, length):
    squared = z_terms[0][:, None, None] + y_terms[0][None, :, None] + x_terms[0][None, None, :]
    anchor = squared == 0.0
    safe_squared = jnp.where(anchor, 1.0, squared)
    damped = jnp.exp(squared * (-(math.pi * math.pi) / (EWALD_SPLIT * EWALD_SPLIT))) / (
        safe_squared * (math.pi * (length * NY * NX))
    )
    fixes = z_terms[1][:, None, None] * y_terms[1][None, :, None] * x_terms[1][None, None, :]
    return jnp.where(anchor, 0.0, damped) * fixes


def tables(length):
    steps = np.arange(length)
    angles = (steps[:, None] * steps[None, :] % length) * (FULL_TURN / length)
    return np.cos(angles).astype(np.float32), np.sin(angles).astype(np.float32)


def transform_by_steps(grid, rows):
    pencils = lax.axis_size("pencil")
    tiles, _, _, _ = grid.shape
    cosine, sine = tables(NX)
    both = np.stack([cosine, -sine], axis=1).reshape(tiles, LANES, 2, NX)
    after_x = jnp.einsum("tzrl,tlck->czrk", grid, both, precision=HIGH)
    got = lax.all_to_all(after_x[:, None], "pencil", split_axis=4, concat_axis=1, tiled=True)
    rim = jnp.roll(got[:, :, :, :RIM], -1, axis=1)
    body = got[:, :, :, RIM:]
    body = jnp.concatenate([body[:, :, :, : rows - RIM], body[:, :, :, rows - RIM :] + rim], axis=3)
    cosine, sine = tables(NY)
    shape = (pencils, rows, NY)
    turn = np.stack([np.stack([cosine, sine]), np.stack([-sine, cosine])])
    turn = turn.reshape(2, 2, *shape)
    after_y = jnp.einsum("dcprk,cpzrx->dzkx", turn, body, precision=HIGH)
    got = lax.all_to_all(after_y, "brick", split_axis=2, concat_axis=1, tiled=True)
    length = got.shape[1]
    cosine, sine = tables(length)
    turn = np.stack([np.stack([cosine, sine]), np.stack([-sine, cosine])])
    transformed = jnp.einsum("dczk,czyx->dkyx", turn, got, precision=HIGH)
    row_part = transformed.shape[2]
    column_part = transformed.shape[3]
    wave_depth = jnp.arange(length, dtype=jnp.int32)
    wave_rows = lax.axis_index("brick") * row_part + jnp.arange(row_part, dtype=jnp.int32)
    wave_columns = lax.axis_index("pencil") * column_part + jnp.arange(column_part, dtype=jnp.int32)
    kernel = ewald_kernel(
        terms_of(wave_depth, length), terms_of(wave_rows, NY), terms_of(wave_columns, NX), length
    )
    power = transformed[0] * transformed[0] + transformed[1] * transformed[1]
    total = lax.psum(jnp.sum(kernel * power), ("brick", "pencil"))
    return total.reshape(1), transformed


def wave_terms(length):
    wave = np.arange(length)
    fraction = np.where(2 * wave >= length, wave - length, wave) / length
    fix = 9.0 / (2.0 + np.cos(wave * (FULL_TURN / length))) ** 2
    weight = fix * np.exp(-(math.pi**2) / EWALD_SPLIT**2 * fraction**2)
    return (fraction**2).astype(np.float32), weight.astype(np.float32)


def by_factor(value, angle):
    cosine, sine = math.cos(angle), math.sin(angle)
    real, imag = value
    if abs(sine) < 1e-12 and cosine > 0.0:
        return value
    if abs(cosine) < 1e-12 and sine > 0.0:
        return imag, -real
    return real * cosine + imag * sine, imag * cosine - real * sine


def radix_two(values):
    count = len(values)
    if count == 1:
        return values
    even, odd = radix_two(values[0::2]), radix_two(values[1::2])
    odd = [by_factor(value, FULL_TURN * k / count) for k, value in enumerate(odd)]
    first = [(a[0] + b[0], a[1] + b[1]) for a, b in zip(even, odd)]
    return first + [(a[0] - b[0], a[1] - b[1]) for a, b in zip(even, odd)]


def leading_transform(parts):
    bricks = len(parts[0])
    length = ZDEV * bricks
    result = [None] * length
    for k in range(bricks):
        base = parts[0][k]
        one = by_factor(parts[1][k], FULL_TURN * k / length)
        two = by_factor(parts[2][k], FULL_TURN * 2 * k / length)
        total = (one[0] + two[0], one[1] + two[1])
        apart = ((one[0] - two[0]) * (0.5 * math.sqrt(3.0)), (one[1] - two[1]) * (0.5 * math.sqrt(3.0)))
        middle = (base[0] - 0.5 * total[0], base[1] - 0.5 * total[1])
        result[k] = (base[0] + total[0], base[1] + total[1])
        result[k + bricks] = (middle[0] + apart[1], middle[1] - apart[0])
        result[k + 2 * bricks] = (middle[0] - apart[1], middle[1] + apart[0])
    return result


def fused_kernel(
    pencils, bricks,
    grid_ref, high_ref, low_ref, yterm_ref, xterm_ref,
    energy_ref, spectrum_ref,
    xs, xr, ys, zr, ep, eb,
    xsend, xrecv, zsend, zrecv, epsend, eprecv, ebsend, ebrecv,
):
    mine = {"pencil": lax.axis_index("pencil"), "brick": lax.axis_index("brick")}
    sizes = {"pencil": pencils, "brick": bricks}
    part = NY // bricks
    rows = NY // pencils
    started = []

    def peer(axis, step):
        half = sizes[axis] // 2
        side, place = mine[axis] // half, mine[axis] % half
        if step <= half:
            return (1 - side) * half + lax.rem(place + step - 1, half)
        return side * half + lax.rem(place + step - half, half)

    def send(axis, step, source, target, send_sem, recv_sem):
        copy = pltpu.make_async_remote_copy(
            src_ref=source, dst_ref=target, send_sem=send_sem, recv_sem=recv_sem,
            device_id={axis: peer(axis, step)}, device_id_type=pl.DeviceIdType.MESH,
        )
        copy.start()
        started.append(copy)

    def arrived(axis, step, target, recv_sem, send_sem):
        pltpu.make_async_remote_copy(
            src_ref=target, dst_ref=target, send_sem=send_sem, recv_sem=recv_sem,
            device_id={axis: peer(axis, step)}, device_id_type=pl.DeviceIdType.MESH,
        ).wait_recv()

    barrier = pltpu.get_barrier_semaphore()
    for axis in sizes:
        for step in range(1, sizes[axis]):
            pl.semaphore_signal(
                barrier, inc=1, device_id={axis: peer(axis, step)},
                device_id_type=pl.DeviceIdType.MESH,
            )

    me, slab = mine["pencil"], mine["brick"]

    def send_lines(plane):
        for step in range(1, pencils):
            send(
                "pencil", step, xs.at[plane, peer("pencil", step)], xr.at[plane, me],
                xsend.at[plane, step], xrecv.at[plane, me],
            )

    for plane in range(ZDEV):
        lines = jnp.concatenate([grid_ref[t, plane] for t in range(NX // LANES)], axis=1)
        lines = split(lines)
        real = dot3(lines, (high_ref[0:NX], low_ref[0:NX]), ((1,), (0,)))
        imag = -dot3(lines, (high_ref[NX:], low_ref[NX:]), ((1,), (0,)))
        for target in range(pencils):
            xs[plane, target, :, 0:LANES] = real[:, target * LANES : (target + 1) * LANES]
            xs[plane, target, :, LANES:] = imag[:, target * LANES : (target + 1) * LANES]
        if plane == 0:
            pl.semaphore_wait(barrier, pencils + bricks - 2)
            send_lines(plane)
        xr[plane, me] = xs[plane, me]

    for plane in range(ZDEV):
        for step in range(1, pencils):
            other = peer("pencil", step)
            arrived("pencil", step, xr.at[plane, other], xrecv.at[plane, other], xsend.at[plane, step])
        if plane + 1 < ZDEV:
            send_lines(plane + 1)
        pieces = []
        for source in range(pencils):
            pieces.append(xr[plane, source, RIM:rows])
            rim = xr[plane, (source + 1) % pencils, 0:RIM]
            pieces.append(xr[plane, source, rows : rows + RIM] + rim)
        columns = split(jnp.concatenate(pieces, axis=0))
        both = dot3((high_ref[...], low_ref[...]), columns, ((1,), (0,)))
        real = both[:NY, :LANES] + both[NY:, LANES:]
        imag = both[:NY, LANES:] - both[NY:, :LANES]
        for target in range(bricks):
            ys[plane, target, :, 0:LANES] = real[target * part : (target + 1) * part]
            ys[plane, target, :, LANES:] = imag[target * part : (target + 1) * part]
        for step in range(1, bricks):
            send(
                "brick", step, ys.at[plane, peer("brick", step)], zr.at[plane, slab],
                zsend.at[plane, step], zrecv.at[plane, slab],
            )
        zr[plane, slab] = ys[plane, slab]

    def over_bricks(plane, step, carry):
        here = pl.ds(pl.multiple_of(step * 8, 8), 8)
        values = [
            (zr[plane, b, here, 0:LANES], zr[plane, b, here, LANES : 2 * LANES])
            for b in range(bricks)
        ]
        for k, (real, imag) in enumerate(radix_two(values)):
            zr[plane, k, here, 0:LANES] = real
            zr[plane, k, here, LANES : 2 * LANES] = imag
        return carry

    for plane in range(ZDEV):
        for step in range(1, bricks):
            other = peer("brick", step)
            arrived("brick", step, zr.at[plane, other], zrecv.at[plane, other], zsend.at[plane, step])
        if plane + 1 < ZDEV:
            lax.fori_loop(0, part // 8, functools.partial(over_bricks, plane), 0)

    length = ZDEV * bricks
    depth_square, depth_weight = wave_terms(length)
    lanes = pl.ds(pl.multiple_of(me * LANES, LANES), LANES)

    def chunk(step, total):
        here = pl.ds(pl.multiple_of(step * 8, 8), 8)
        planes = [
            [(zr[i, b, here, 0:LANES], zr[i, b, here, LANES : 2 * LANES]) for b in range(bricks)]
            for i in range(ZDEV)
        ]
        result = leading_transform(planes[:-1] + [radix_two(planes[-1])])
        across = pl.ds(pl.multiple_of(slab * part + step * 8, 8), 8)
        square = yterm_ref[0, across, :] + xterm_ref[0, :, lanes]
        weight = yterm_ref[1, across, :] * xterm_ref[1, :, lanes]
        powers = {}
        for k, (real, imag) in enumerate(result):
            spectrum_ref[0, k, here, :] = real
            spectrum_ref[1, k, here, :] = imag
            fold = min(k, length - k)
            powers[fold] = powers.get(fold, 0.0) + (real * real + imag * imag)
        inner = jnp.zeros_like(total)
        for k, power in powers.items():
            q = square + float(depth_square[k])
            term = float(depth_weight[k]) * power / jnp.where(q == 0.0, 1.0, q)
            inner = inner + (jnp.where(q == 0.0, 0.0, term) if k == 0 else term)
        return total + inner * weight

    share = lax.fori_loop(0, part // 8, chunk, jnp.zeros((8, LANES), jnp.float32))
    share = share * (1.0 / (math.pi * (length * NY * NX)))
    for axis, held, sends, recvs in (
        ("pencil", ep, epsend, eprecv), ("brick", eb, ebsend, ebrecv),
    ):
        own = mine[axis]
        held[own] = share
        for step in range(1, sizes[axis]):
            send(axis, step, held.at[own], held.at[own], sends.at[step], recvs.at[own])
        for step in range(1, sizes[axis]):
            other = peer(axis, step)
            arrived(axis, step, held.at[other], recvs.at[other], sends.at[step])
        share = held[0]
        for source in range(1, sizes[axis]):
            share = share + held[source]
    energy_ref[...] = share
    for copy in started:
        copy.wait_send()


def transform_fused(grid, rows):
    pencils, bricks = lax.axis_size("pencil"), lax.axis_size("brick")
    part = NY // bricks
    columns = NX // pencils
    cosine, sine = tables(NY)
    turn_y = np.concatenate([cosine, sine], axis=0)

    def halves(table):
        high = table.astype(jnp.bfloat16)
        return high, (table - high.astype(np.float32)).astype(jnp.bfloat16)

    y_terms = np.broadcast_to(np.stack(wave_terms(NY))[:, :, None], (2, NY, LANES))
    x_terms = np.broadcast_to(np.stack(wave_terms(NX))[:, None, :], (2, 8, NX))
    f32 = jnp.float32
    whole = pl.BlockSpec(memory_space=pltpu.VMEM)
    dma = pltpu.SemaphoreType.DMA
    energy, spectrum = pl.pallas_call(
        functools.partial(fused_kernel, pencils, bricks),
        out_shape=(
            jax.ShapeDtypeStruct((8, LANES), f32),
            jax.ShapeDtypeStruct((2, ZDEV * bricks, part, columns), f32),
        ),
        in_specs=[whole] * 5,
        out_specs=(whole, whole),
        scratch_shapes=[
            pltpu.VMEM((ZDEV, pencils, rows + RIM, 2 * LANES), f32),
            pltpu.VMEM((ZDEV, pencils, rows + RIM, 2 * LANES), f32),
            pltpu.VMEM((ZDEV, bricks, part, 2 * LANES), f32),
            pltpu.VMEM((ZDEV, bricks, part, 2 * LANES), f32),
            pltpu.VMEM((pencils, 8, LANES), f32),
            pltpu.VMEM((bricks, 8, LANES), f32),
            dma((ZDEV, pencils)), dma((ZDEV, pencils)),
            dma((ZDEV, bricks)), dma((ZDEV, bricks)),
            dma((pencils,)), dma((pencils,)), dma((bricks,)), dma((bricks,)),
        ],
        compiler_params=pltpu.CompilerParams(
            collective_id=0, has_side_effects=True, vmem_limit_bytes=24 * 1024 * 1024
        ),
        cost_estimate=pl.CostEstimate(
            flops=6_000_000_000, bytes_accessed=8_000_000, transcendentals=0
        ),
    )(grid, *halves(turn_y), y_terms.astype(np.float32), x_terms.astype(np.float32))
    return jnp.sum(energy).reshape(1), spectrum


def shards(positions, charges, anchor_row, anchor_column, counts):
    slot_count = anchor_row.shape[0]
    atoms = charges.shape[0]
    rows = NY // lax.axis_size("pencil")
    coords = jnp.concatenate([positions, charges.reshape(1, atoms)], axis=0)
    anchors = jnp.concatenate([anchor_row, anchor_column, counts])
    far_anchors, far_coords = (from_behind(array, "brick", -1) for array in (anchors, coords))
    grid = spread(3, rows, anchors, coords)
    grid = spread(0, rows, far_anchors, far_coords, grid)
    bricks = lax.axis_size("brick")
    tiled = NX // lax.axis_size("pencil") == LANES and NY // bricks % 8 == 0
    if tiled and bricks & (bricks - 1) == 0:
        total, spectrum = transform_fused(grid, rows)
    else:
        total, spectrum = transform_by_steps(grid, rows)
    slot_total = slot_count * lax.axis_size("brick") * lax.axis_size("pencil")
    return (total * (0.5 / slot_total), spectrum)


def solution(mesh):
    return jax.shard_map(
        shards,
        mesh=mesh,
        in_specs=(
            P(None, ("brick", "pencil")),
            P(("brick", "pencil")),
            P(("brick", "pencil")),
            P(("brick", "pencil")),
            P(("brick", "pencil")),
        ),
        out_specs=(P(), P(None, None, "brick", "pencil")),
        check_vma=False,
    )
```

```python
import functools
import math

import jax
import jax.numpy as jnp
import numpy as np
from jax import lax
from jax.experimental import pallas as pl
from jax.experimental.pallas import tpu as pltpu
from jax.sharding import PartitionSpec as P

NX = 512
NY = 512
ZDEV = 3
PY = 16
PX = 16
LANES = 128
RIM = 8
GROUP = 4

FULL_TURN = 2.0 * math.pi
EWALD_SPLIT = 0.35
HIGH = lax.Precision.HIGH


def from_behind(block, axis, distance):
    devices = range(lax.axis_size(axis))
    route = [((i - distance) % len(devices), i) for i in devices]
    return lax.ppermute(block, axis, route)


def spline(offset):
    distance = jnp.abs(offset - 2.0)
    outer = jnp.maximum(2.0 - distance, 0.0)
    inner = jnp.maximum(1.0 - distance, 0.0)
    return (outer * outer * outer - 4.0 * (inner * inner * inner)) * (1.0 / 6.0)


def split(value):
    high = value.astype(jnp.bfloat16)
    low = (value - high.astype(jnp.float32)).astype(jnp.bfloat16)
    return high, low


def dot3(left, right, dims):
    def one(a, b):
        return lax.dot_general(a, b, (dims, ((), ())), preferred_element_type=jnp.float32)

    return one(left[0], right[1]) + one(left[1], right[0]) + one(left[0], right[0])


def spread_kernel(first_plane, block_atoms, *refs):
    anchor_ref, coords_ref, *before, grid_ref = refs
    slots = anchor_ref.shape[0] // 2
    count = anchor_ref[2 * slots]
    if before:
        grid_ref[...] = before[0][...]
    else:
        grid_ref[...] = jnp.zeros_like(grid_ref)
    tiles = grid_ref.shape[0]
    width = GROUP * block_atoms
    lane_block = lax.broadcasted_iota(jnp.int32, (PY, width), 1) // block_atoms
    steps = lax.broadcasted_iota(jnp.int32, (PY, width), 0).astype(jnp.float32)
    planes = (lax.broadcasted_iota(jnp.int32, (8, width), 0) + first_plane).astype(jnp.float32)
    lane = lax.broadcasted_iota(jnp.int32, (ZDEV * PY, LANES), 1)
    blank = jnp.zeros((LANES - PX, width), jnp.bfloat16)

    def turn(step, carry):
        here = pl.ds(pl.multiple_of(step * width, width), width)
        live = lane_block[0:1] + step * GROUP < count
        charge = jnp.where(live, coords_ref[3:4, here], 0.0)
        depth = spline(coords_ref[0:1, here] - planes) * charge
        lines = spline(coords_ref[1:2, here] - steps)
        cells = split(spline(coords_ref[2:3, here] - steps))
        cells = [jnp.concatenate([part, blank], axis=0) for part in cells]
        pieces = []
        for member in range(GROUP):
            own = jnp.where(lane_block == member, lines, 0.0)
            for plane in range(ZDEV):
                pieces.append(split(own * depth[plane : plane + 1]))
        sheets = [jnp.concatenate([piece[i] for piece in pieces], axis=0) for i in range(2)]
        values = dot3(sheets, cells, ((1,), (1,)))
        for member in range(GROUP):
            block = step * GROUP + member
            column = anchor_ref[slots + block]
            row = anchor_ref[block] + (RIM - 3)
            shift = column & (LANES - 1)
            tile = column // LANES
            over = (tile + 1) & (tiles - 1)
            patch = values[member * ZDEV * PY : (member + 1) * ZDEV * PY]
            patch = pltpu.roll(patch, shift, 1)
            parts = (
                (tile, jnp.where(lane >= shift, patch, 0.0)),
                (over, jnp.where(lane >= shift, 0.0, patch)),
            )
            sums = []
            for where, part in parts:
                for plane in range(ZDEV):
                    old = grid_ref[where, plane, pl.ds(row, PY), :]
                    sums.append(old + part[plane * PY : (plane + 1) * PY])
            for index, (where, part) in enumerate(parts):
                for plane in range(ZDEV):
                    grid_ref[where, plane, pl.ds(row, PY), :] = sums[index * ZDEV + plane]
        return carry

    lax.fori_loop(0, slots // GROUP, turn, 0, unroll=4)


def spread(first_plane, rows, anchors, coords, *before):
    slots = anchors.shape[0] // 2
    shape = (NX // LANES, ZDEV, rows + RIM, LANES)
    scalar = pl.BlockSpec(memory_space=pltpu.SMEM)
    whole = pl.BlockSpec(memory_space=pltpu.VMEM)
    return pl.pallas_call(
        functools.partial(spread_kernel, first_plane, coords.shape[1] // slots),
        out_shape=jax.ShapeDtypeStruct(shape, jnp.float32),
        in_specs=[scalar] + [whole] * (1 + len(before)),
        out_specs=whole,
        compiler_params=pltpu.CompilerParams(vmem_limit_bytes=10 * 1024 * 1024),
        cost_estimate=pl.CostEstimate(
            flops=20_000_000, bytes_accessed=4_000_000, transcendentals=0
        ),
    )(anchors, coords, *before)


def terms_of(wave_index, length):
    signed = jnp.where(2 * wave_index >= length, wave_index - length, wave_index)
    fraction = signed.astype(jnp.float32) / length
    cosine = jnp.cos(wave_index.astype(jnp.float32) * (FULL_TURN / length))
    spline_fix = 9.0 / ((2.0 + cosine) * (2.0 + cosine))
    return (fraction * fraction, spline_fix)


def ewald_kernel(z_terms, y_terms, x_terms, length):
    squared = z_terms[0][:, None, None] + y_terms[0][None, :, None] + x_terms[0][None, None, :]
    anchor = squared == 0.0
    safe_squared = jnp.where(anchor, 1.0, squared)
    damped = jnp.exp(squared * (-(math.pi * math.pi) / (EWALD_SPLIT * EWALD_SPLIT))) / (
        safe_squared * (math.pi * (length * NY * NX))
    )
    fixes = z_terms[1][:, None, None] * y_terms[1][None, :, None] * x_terms[1][None, None, :]
    return jnp.where(anchor, 0.0, damped) * fixes


def tables(length):
    steps = np.arange(length)
    angles = (steps[:, None] * steps[None, :] % length) * (FULL_TURN / length)
    return np.cos(angles).astype(np.float32), np.sin(angles).astype(np.float32)


def transform_by_steps(grid, rows):
    pencils = lax.axis_size("pencil")
    tiles, _, _, _ = grid.shape
    cosine, sine = tables(NX)
    both = np.stack([cosine, -sine], axis=1).reshape(tiles, LANES, 2, NX)
    after_x = jnp.einsum("tzrl,tlck->czrk", grid, both, precision=HIGH)
    got = lax.all_to_all(after_x[:, None], "pencil", split_axis=4, concat_axis=1, tiled=True)
    rim = jnp.roll(got[:, :, :, :RIM], -1, axis=1)
    body = got[:, :, :, RIM:]
    body = jnp.concatenate([body[:, :, :, : rows - RIM], body[:, :, :, rows - RIM :] + rim], axis=3)
    cosine, sine = tables(NY)
    shape = (pencils, rows, NY)
    turn = np.stack([np.stack([cosine, sine]), np.stack([-sine, cosine])])
    turn = turn.reshape(2, 2, *shape)
    after_y = jnp.einsum("dcprk,cpzrx->dzkx", turn, body, precision=HIGH)
    got = lax.all_to_all(after_y, "brick", split_axis=2, concat_axis=1, tiled=True)
    length = got.shape[1]
    cosine, sine = tables(length)
    turn = np.stack([np.stack([cosine, sine]), np.stack([-sine, cosine])])
    transformed = jnp.einsum("dczk,czyx->dkyx", turn, got, precision=HIGH)
    row_part = transformed.shape[2]
    column_part = transformed.shape[3]
    wave_depth = jnp.arange(length, dtype=jnp.int32)
    wave_rows = lax.axis_index("brick") * row_part + jnp.arange(row_part, dtype=jnp.int32)
    wave_columns = lax.axis_index("pencil") * column_part + jnp.arange(column_part, dtype=jnp.int32)
    kernel = ewald_kernel(
        terms_of(wave_depth, length), terms_of(wave_rows, NY), terms_of(wave_columns, NX), length
    )
    power = transformed[0] * transformed[0] + transformed[1] * transformed[1]
    total = lax.psum(jnp.sum(kernel * power), ("brick", "pencil"))
    return total.reshape(1), transformed


def wave_terms(length):
    wave = np.arange(length)
    fraction = np.where(2 * wave >= length, wave - length, wave) / length
    fix = 9.0 / (2.0 + np.cos(wave * (FULL_TURN / length))) ** 2
    weight = fix * np.exp(-(math.pi**2) / EWALD_SPLIT**2 * fraction**2)
    return (fraction**2).astype(np.float32), weight.astype(np.float32)


def by_factor(value, angle):
    cosine, sine = math.cos(angle), math.sin(angle)
    real, imag = value
    if abs(sine) < 1e-12 and cosine > 0.0:
        return value
    if abs(cosine) < 1e-12 and sine > 0.0:
        return imag, -real
    return real * cosine + imag * sine, imag * cosine - real * sine


def radix_two(values):
    count = len(values)
    if count == 1:
        return values
    even, odd = radix_two(values[0::2]), radix_two(values[1::2])
    odd = [by_factor(value, FULL_TURN * k / count) for k, value in enumerate(odd)]
    first = [(a[0] + b[0], a[1] + b[1]) for a, b in zip(even, odd)]
    return first + [(a[0] - b[0], a[1] - b[1]) for a, b in zip(even, odd)]


def leading_transform(parts):
    bricks = len(parts[0])
    length = ZDEV * bricks
    result = [None] * length
    for k in range(bricks):
        base = parts[0][k]
        one = by_factor(parts[1][k], FULL_TURN * k / length)
        two = by_factor(parts[2][k], FULL_TURN * 2 * k / length)
        total = (one[0] + two[0], one[1] + two[1])
        apart = ((one[0] - two[0]) * (0.5 * math.sqrt(3.0)), (one[1] - two[1]) * (0.5 * math.sqrt(3.0)))
        middle = (base[0] - 0.5 * total[0], base[1] - 0.5 * total[1])
        result[k] = (base[0] + total[0], base[1] + total[1])
        result[k + bricks] = (middle[0] + apart[1], middle[1] - apart[0])
        result[k + 2 * bricks] = (middle[0] - apart[1], middle[1] + apart[0])
    return result


def fused_kernel(
    pencils, bricks,
    grid_ref, high_ref, low_ref, yterm_ref, xterm_ref,
    energy_ref, spectrum_ref,
    xs, xr, ys, zr, xs0, xr0, ys0, zr0, zd, ep, eb,
    xsend, xrecv, zsend, zrecv, xsend0, xrecv0, zsend0, zrecv0, epsend, eprecv, ebsend, ebrecv,
):
    mine = {"pencil": lax.axis_index("pencil"), "brick": lax.axis_index("brick")}
    sizes = {"pencil": pencils, "brick": bricks}
    part = NY // bricks
    rows = NY // pencils
    started = []

    def peer(axis, step):
        half = sizes[axis] // 2
        side, place = mine[axis] // half, mine[axis] % half
        if step <= half:
            return (1 - side) * half + lax.rem(place + step - 1, half)
        return side * half + lax.rem(place + step - half, half)

    def send(axis, step, source, target, send_sem, recv_sem):
        copy = pltpu.make_async_remote_copy(
            src_ref=source, dst_ref=target, send_sem=send_sem, recv_sem=recv_sem,
            device_id={axis: peer(axis, step)}, device_id_type=pl.DeviceIdType.MESH,
        )
        copy.start()
        started.append(copy)

    def arrived(axis, step, target, recv_sem, send_sem):
        pltpu.make_async_remote_copy(
            src_ref=target, dst_ref=target, send_sem=send_sem, recv_sem=recv_sem,
            device_id={axis: peer(axis, step)}, device_id_type=pl.DeviceIdType.MESH,
        ).wait_recv()

    barrier = pltpu.get_barrier_semaphore()
    for axis in sizes:
        for step in range(1, sizes[axis]):
            pl.semaphore_signal(
                barrier, inc=1, device_id={axis: peer(axis, step)},
                device_id_type=pl.DeviceIdType.MESH,
            )

    me, slab = mine["pencil"], mine["brick"]

    half = LANES // 2

    def send_first(part_index):
        for step in range(1, pencils):
            send(
                "pencil", step, xs0.at[part_index, peer("pencil", step)], xr0.at[part_index, me],
                xsend0.at[part_index, step], xrecv0.at[part_index, me],
            )

    def in_halves(real, imag):
        low = lax.broadcasted_iota(jnp.int32, real.shape, 1) < half
        return (
            jnp.where(low, real, pltpu.roll(imag, half, 1)),
            jnp.where(low, pltpu.roll(real, half, 1), imag),
        )

    def send_lines(plane):
        for step in range(1, pencils):
            send(
                "pencil", step, xs.at[plane, peer("pencil", step)], xr.at[plane, me],
                xsend.at[plane, step], xrecv.at[plane, me],
            )

    for plane in range(ZDEV):
        lines = jnp.concatenate([grid_ref[t, plane] for t in range(NX // LANES)], axis=1)
        lines = split(lines)
        real = dot3(lines, (high_ref[0:NX], low_ref[0:NX]), ((1,), (0,)))
        imag = -dot3(lines, (high_ref[NX:], low_ref[NX:]), ((1,), (0,)))
        if plane == 0:
            for target in range(pencils):
                own = slice(target * LANES, (target + 1) * LANES)
                xs0[0, target], xs0[1, target] = in_halves(real[:, own], imag[:, own])
            pl.semaphore_wait(barrier, pencils + bricks - 2)
            send_first(0)
            xr0[0, me] = xs0[0, me]
            xr0[1, me] = xs0[1, me]
            continue
        for target in range(pencils):
            xs[plane - 1, target, :, 0:LANES] = real[:, target * LANES : (target + 1) * LANES]
            xs[plane - 1, target, :, LANES:] = imag[:, target * LANES : (target + 1) * LANES]
        xr[plane - 1, me] = xs[plane - 1, me]

    def gathered(held):
        pieces = []
        for source in range(pencils):
            pieces.append(held[source, RIM:rows])
            pieces.append(held[source, rows : rows + RIM] + held[(source + 1) % pencils, 0:RIM])
        return split(jnp.concatenate(pieces, axis=0))

    for index in range(2):
        for step in range(1, pencils):
            other = peer("pencil", step)
            arrived(
                "pencil", step, xr0.at[index, other], xrecv0.at[index, other], xsend0.at[index, step]
            )
        if index == 0:
            send_first(1)
        else:
            send_lines(0)
        both = dot3((high_ref[...], low_ref[...]), gathered(xr0.at[index]), ((1,), (0,)))
        turned = pltpu.roll(both[NY:], half, 1)
        low = lax.broadcasted_iota(jnp.int32, turned.shape, 1) < half
        both = both[:NY] + jnp.where(low, turned, -turned)
        for target in range(bricks):
            ys0[index, target] = both[target * part : (target + 1) * part]
        for step in range(1, bricks):
            send(
                "brick", step, ys0.at[index, peer("brick", step)], zr0.at[index, slab],
                zsend0.at[index, step], zrecv0.at[index, slab],
            )
        zr0[index, slab] = ys0[index, slab]

    for plane in range(ZDEV - 1):
        for step in range(1, pencils):
            other = peer("pencil", step)
            arrived("pencil", step, xr.at[plane, other], xrecv.at[plane, other], xsend.at[plane, step])
        if plane + 1 < ZDEV - 1:
            send_lines(plane + 1)
        columns = gathered(xr.at[plane])
        both = dot3((high_ref[...], low_ref[...]), columns, ((1,), (0,)))
        real = both[:NY, :LANES] + both[NY:, LANES:]
        imag = both[:NY, LANES:] - both[NY:, :LANES]
        for target in range(bricks):
            ys[plane, target, :, 0:LANES] = real[target * part : (target + 1) * part]
            ys[plane, target, :, LANES:] = imag[target * part : (target + 1) * part]
        for step in range(1, bricks):
            send(
                "brick", step, ys.at[plane, peer("brick", step)], zr.at[plane, slab],
                zsend.at[plane, step], zrecv.at[plane, slab],
            )
        zr[plane, slab] = ys[plane, slab]

    def over_bricks(plane, step, carry):
        here = pl.ds(pl.multiple_of(step * 8, 8), 8)
        if plane == 0:
            values = [in_halves(zr0[0, b, here, :], zr0[1, b, here, :]) for b in range(bricks)]
        else:
            values = [
                (zr[0, b, here, 0:LANES], zr[0, b, here, LANES : 2 * LANES]) for b in range(bricks)
            ]
        for k, (real, imag) in enumerate(radix_two(values)):
            zd[plane, k, here, 0:LANES] = real
            zd[plane, k, here, LANES : 2 * LANES] = imag
        return carry

    for index in range(2):
        for step in range(1, bricks):
            other = peer("brick", step)
            arrived(
                "brick", step, zr0.at[index, other], zrecv0.at[index, other], zsend0.at[index, step]
            )
    for plane in range(ZDEV):
        if plane > 0:
            for step in range(1, bricks):
                other = peer("brick", step)
                arrived(
                    "brick", step, zr.at[plane - 1, other], zrecv.at[plane - 1, other],
                    zsend.at[plane - 1, step],
                )
        if plane + 1 < ZDEV:
            lax.fori_loop(0, part // 8, functools.partial(over_bricks, plane), 0)

    length = ZDEV * bricks
    depth_square, depth_weight = wave_terms(length)
    lanes = pl.ds(pl.multiple_of(me * LANES, LANES), LANES)

    def chunk(step, total):
        here = pl.ds(pl.multiple_of(step * 8, 8), 8)
        planes = [
            [(held[i, b, here, 0:LANES], held[i, b, here, LANES : 2 * LANES]) for b in range(bricks)]
            for held, i in ((zd, 0), (zd, 1), (zr, 1))
        ]
        result = leading_transform(planes[:-1] + [radix_two(planes[-1])])
        across = pl.ds(pl.multiple_of(slab * part + step * 8, 8), 8)
        square = yterm_ref[0, across, :] + xterm_ref[0, :, lanes]
        weight = yterm_ref[1, across, :] * xterm_ref[1, :, lanes]
        powers = {}
        for k, (real, imag) in enumerate(result):
            spectrum_ref[0, k, here, :] = real
            spectrum_ref[1, k, here, :] = imag
            fold = min(k, length - k)
            powers[fold] = powers.get(fold, 0.0) + (real * real + imag * imag)
        inner = jnp.zeros_like(total)
        for k, power in powers.items():
            q = square + float(depth_square[k])
            term = float(depth_weight[k]) * power / jnp.where(q == 0.0, 1.0, q)
            inner = inner + (jnp.where(q == 0.0, 0.0, term) if k == 0 else term)
        return total + inner * weight

    share = lax.fori_loop(0, part // 8, chunk, jnp.zeros((8, LANES), jnp.float32))
    share = share * (1.0 / (math.pi * (length * NY * NX)))
    for axis, held, sends, recvs in (
        ("pencil", ep, epsend, eprecv), ("brick", eb, ebsend, ebrecv),
    ):
        own = mine[axis]
        held[own] = share
        for step in range(1, sizes[axis]):
            send(axis, step, held.at[own], held.at[own], sends.at[step], recvs.at[own])
        for step in range(1, sizes[axis]):
            other = peer(axis, step)
            arrived(axis, step, held.at[other], recvs.at[other], sends.at[step])
        share = held[0]
        for source in range(1, sizes[axis]):
            share = share + held[source]
    energy_ref[...] = share
    for copy in started:
        copy.wait_send()


def transform_fused(grid, rows):
    pencils, bricks = lax.axis_size("pencil"), lax.axis_size("brick")
    part = NY // bricks
    columns = NX // pencils
    cosine, sine = tables(NY)
    turn_y = np.concatenate([cosine, sine], axis=0)

    def halves(table):
        high = table.astype(jnp.bfloat16)
        return high, (table - high.astype(np.float32)).astype(jnp.bfloat16)

    y_terms = np.broadcast_to(np.stack(wave_terms(NY))[:, :, None], (2, NY, LANES))
    x_terms = np.broadcast_to(np.stack(wave_terms(NX))[:, None, :], (2, 8, NX))
    f32 = jnp.float32
    whole = pl.BlockSpec(memory_space=pltpu.VMEM)
    dma = pltpu.SemaphoreType.DMA
    energy, spectrum = pl.pallas_call(
        functools.partial(fused_kernel, pencils, bricks),
        out_shape=(
            jax.ShapeDtypeStruct((8, LANES), f32),
            jax.ShapeDtypeStruct((2, ZDEV * bricks, part, columns), f32),
        ),
        in_specs=[whole] * 5,
        out_specs=(whole, whole),
        scratch_shapes=[
            pltpu.VMEM((ZDEV - 1, pencils, rows + RIM, 2 * LANES), f32),
            pltpu.VMEM((ZDEV - 1, pencils, rows + RIM, 2 * LANES), f32),
            pltpu.VMEM((ZDEV - 1, bricks, part, 2 * LANES), f32),
            pltpu.VMEM((ZDEV - 1, bricks, part, 2 * LANES), f32),
            pltpu.VMEM((2, pencils, rows + RIM, LANES), f32),
            pltpu.VMEM((2, pencils, rows + RIM, LANES), f32),
            pltpu.VMEM((2, bricks, part, LANES), f32),
            pltpu.VMEM((2, bricks, part, LANES), f32),
            pltpu.VMEM((2, bricks, part, 2 * LANES), f32),
            pltpu.VMEM((pencils, 8, LANES), f32),
            pltpu.VMEM((bricks, 8, LANES), f32),
            dma((ZDEV, pencils)), dma((ZDEV, pencils)),
            dma((ZDEV, bricks)), dma((ZDEV, bricks)),
            dma((2, pencils)), dma((2, pencils)),
            dma((2, bricks)), dma((2, bricks)),
            dma((pencils,)), dma((pencils,)), dma((bricks,)), dma((bricks,)),
        ],
        compiler_params=pltpu.CompilerParams(
            collective_id=0, has_side_effects=True, vmem_limit_bytes=24 * 1024 * 1024
        ),
        cost_estimate=pl.CostEstimate(
            flops=6_000_000_000, bytes_accessed=8_000_000, transcendentals=0
        ),
    )(grid, *halves(turn_y), y_terms.astype(np.float32), x_terms.astype(np.float32))
    return jnp.sum(energy).reshape(1), spectrum


def shards(positions, charges, anchor_row, anchor_column, counts):
    slot_count = anchor_row.shape[0]
    atoms = charges.shape[0]
    rows = NY // lax.axis_size("pencil")
    coords = jnp.concatenate([positions, charges.reshape(1, atoms)], axis=0)
    anchors = jnp.concatenate([anchor_row, anchor_column, counts])
    far_anchors, far_coords = (from_behind(array, "brick", -1) for array in (anchors, coords))
    grid = spread(3, rows, anchors, coords)
    grid = spread(0, rows, far_anchors, far_coords, grid)
    bricks = lax.axis_size("brick")
    tiled = NX // lax.axis_size("pencil") == LANES and NY // bricks % 8 == 0
    if tiled and bricks & (bricks - 1) == 0:
        total, spectrum = transform_fused(grid, rows)
    else:
        total, spectrum = transform_by_steps(grid, rows)
    slot_total = slot_count * lax.axis_size("brick") * lax.axis_size("pencil")
    return (total * (0.5 / slot_total), spectrum)


def solution(mesh):
    return jax.shard_map(
        shards,
        mesh=mesh,
        in_specs=(
            P(None, ("brick", "pencil")),
            P(("brick", "pencil")),
            P(("brick", "pencil")),
            P(("brick", "pencil")),
            P(("brick", "pencil")),
        ),
        out_specs=(P(), P(None, None, "brick", "pencil")),
        check_vma=False,
    )
```

```python
import functools
import math

import jax
import jax.numpy as jnp
import numpy as np
from jax import lax
from jax.experimental import pallas as pl
from jax.experimental.pallas import tpu as pltpu
from jax.sharding import PartitionSpec as P

NX = 512
NY = 512
ZDEV = 3
PY = 16
PX = 16
LANES = 128
RIM = 8
GROUP = 4

FULL_TURN = 2.0 * math.pi
EWALD_SPLIT = 0.35
HIGH = lax.Precision.HIGH


def from_behind(block, axis, distance):
    devices = range(lax.axis_size(axis))
    route = [((i - distance) % len(devices), i) for i in devices]
    return lax.ppermute(block, axis, route)


def spline(offset):
    distance = jnp.abs(offset - 2.0)
    outer = jnp.maximum(2.0 - distance, 0.0)
    inner = jnp.maximum(1.0 - distance, 0.0)
    return (outer * outer * outer - 4.0 * (inner * inner * inner)) * (1.0 / 6.0)


def split(value):
    high = value.astype(jnp.bfloat16)
    low = (value - high.astype(jnp.float32)).astype(jnp.bfloat16)
    return high, low


def dot3(left, right, dims):
    def one(a, b):
        return lax.dot_general(a, b, (dims, ((), ())), preferred_element_type=jnp.float32)

    return one(left[0], right[1]) + one(left[1], right[0]) + one(left[0], right[0])


def spread_kernel(first_plane, block_atoms, *refs):
    anchor_ref, coords_ref, *before, grid_ref = refs
    slots = anchor_ref.shape[0] // 2
    count = anchor_ref[2 * slots]
    if before:
        grid_ref[...] = before[0][...]
    else:
        grid_ref[...] = jnp.zeros_like(grid_ref)
    tiles = grid_ref.shape[0]
    width = GROUP * block_atoms
    lane_block = lax.broadcasted_iota(jnp.int32, (PY, width), 1) // block_atoms
    steps = lax.broadcasted_iota(jnp.int32, (PY, width), 0).astype(jnp.float32)
    planes = (lax.broadcasted_iota(jnp.int32, (8, width), 0) + first_plane).astype(jnp.float32)
    lane = lax.broadcasted_iota(jnp.int32, (ZDEV * PY, LANES), 1)
    blank = jnp.zeros((LANES - PX, width), jnp.bfloat16)

    def turn(step, carry):
        here = pl.ds(pl.multiple_of(step * width, width), width)
        live = lane_block[0:1] + step * GROUP < count
        charge = jnp.where(live, coords_ref[3:4, here], 0.0)
        depth = spline(coords_ref[0:1, here] - planes) * charge
        lines = spline(coords_ref[1:2, here] - steps)
        cells = split(spline(coords_ref[2:3, here] - steps))
        cells = [jnp.concatenate([part, blank], axis=0) for part in cells]
        pieces = []
        for member in range(GROUP):
            own = jnp.where(lane_block == member, lines, 0.0)
            for plane in range(ZDEV):
                pieces.append(split(own * depth[plane : plane + 1]))
        sheets = [jnp.concatenate([piece[i] for piece in pieces], axis=0) for i in range(2)]
        values = dot3(sheets, cells, ((1,), (1,)))
        for member in range(GROUP):
            block = step * GROUP + member
            column = anchor_ref[slots + block]
            row = anchor_ref[block] + (RIM - 3)
            shift = column & (LANES - 1)
            tile = column // LANES
            over = (tile + 1) & (tiles - 1)
            patch = values[member * ZDEV * PY : (member + 1) * ZDEV * PY]
            patch = pltpu.roll(patch, shift, 1)
            parts = (
                (tile, jnp.where(lane >= shift, patch, 0.0)),
                (over, jnp.where(lane >= shift, 0.0, patch)),
            )
            sums = []
            for where, part in parts:
                for plane in range(ZDEV):
                    old = grid_ref[where, plane, pl.ds(row, PY), :]
                    sums.append(old + part[plane * PY : (plane + 1) * PY])
            for index, (where, part) in enumerate(parts):
                for plane in range(ZDEV):
                    grid_ref[where, plane, pl.ds(row, PY), :] = sums[index * ZDEV + plane]
        return carry

    lax.fori_loop(0, slots // GROUP, turn, 0, unroll=4)


def spread(first_plane, rows, anchors, coords, *before):
    slots = anchors.shape[0] // 2
    shape = (NX // LANES, ZDEV, rows + RIM, LANES)
    scalar = pl.BlockSpec(memory_space=pltpu.SMEM)
    whole = pl.BlockSpec(memory_space=pltpu.VMEM)
    return pl.pallas_call(
        functools.partial(spread_kernel, first_plane, coords.shape[1] // slots),
        out_shape=jax.ShapeDtypeStruct(shape, jnp.float32),
        in_specs=[scalar] + [whole] * (1 + len(before)),
        out_specs=whole,
        compiler_params=pltpu.CompilerParams(vmem_limit_bytes=10 * 1024 * 1024),
        cost_estimate=pl.CostEstimate(
            flops=20_000_000, bytes_accessed=4_000_000, transcendentals=0
        ),
    )(anchors, coords, *before)


def terms_of(wave_index, length):
    signed = jnp.where(2 * wave_index >= length, wave_index - length, wave_index)
    fraction = signed.astype(jnp.float32) / length
    cosine = jnp.cos(wave_index.astype(jnp.float32) * (FULL_TURN / length))
    spline_fix = 9.0 / ((2.0 + cosine) * (2.0 + cosine))
    return (fraction * fraction, spline_fix)


def ewald_kernel(z_terms, y_terms, x_terms, length):
    squared = z_terms[0][:, None, None] + y_terms[0][None, :, None] + x_terms[0][None, None, :]
    anchor = squared == 0.0
    safe_squared = jnp.where(anchor, 1.0, squared)
    damped = jnp.exp(squared * (-(math.pi * math.pi) / (EWALD_SPLIT * EWALD_SPLIT))) / (
        safe_squared * (math.pi * (length * NY * NX))
    )
    fixes = z_terms[1][:, None, None] * y_terms[1][None, :, None] * x_terms[1][None, None, :]
    return jnp.where(anchor, 0.0, damped) * fixes


def tables(length):
    steps = np.arange(length)
    angles = (steps[:, None] * steps[None, :] % length) * (FULL_TURN / length)
    return np.cos(angles).astype(np.float32), np.sin(angles).astype(np.float32)


def transform_by_steps(grid, rows):
    pencils = lax.axis_size("pencil")
    tiles, _, _, _ = grid.shape
    cosine, sine = tables(NX)
    both = np.stack([cosine, -sine], axis=1).reshape(tiles, LANES, 2, NX)
    after_x = jnp.einsum("tzrl,tlck->czrk", grid, both, precision=HIGH)
    got = lax.all_to_all(after_x[:, None], "pencil", split_axis=4, concat_axis=1, tiled=True)
    rim = jnp.roll(got[:, :, :, :RIM], -1, axis=1)
    body = got[:, :, :, RIM:]
    body = jnp.concatenate([body[:, :, :, : rows - RIM], body[:, :, :, rows - RIM :] + rim], axis=3)
    cosine, sine = tables(NY)
    shape = (pencils, rows, NY)
    turn = np.stack([np.stack([cosine, sine]), np.stack([-sine, cosine])])
    turn = turn.reshape(2, 2, *shape)
    after_y = jnp.einsum("dcprk,cpzrx->dzkx", turn, body, precision=HIGH)
    got = lax.all_to_all(after_y, "brick", split_axis=2, concat_axis=1, tiled=True)
    length = got.shape[1]
    cosine, sine = tables(length)
    turn = np.stack([np.stack([cosine, sine]), np.stack([-sine, cosine])])
    transformed = jnp.einsum("dczk,czyx->dkyx", turn, got, precision=HIGH)
    row_part = transformed.shape[2]
    column_part = transformed.shape[3]
    wave_depth = jnp.arange(length, dtype=jnp.int32)
    wave_rows = lax.axis_index("brick") * row_part + jnp.arange(row_part, dtype=jnp.int32)
    wave_columns = lax.axis_index("pencil") * column_part + jnp.arange(column_part, dtype=jnp.int32)
    kernel = ewald_kernel(
        terms_of(wave_depth, length), terms_of(wave_rows, NY), terms_of(wave_columns, NX), length
    )
    power = transformed[0] * transformed[0] + transformed[1] * transformed[1]
    total = lax.psum(jnp.sum(kernel * power), ("brick", "pencil"))
    return total.reshape(1), transformed


def wave_terms(length):
    wave = np.arange(length)
    fraction = np.where(2 * wave >= length, wave - length, wave) / length
    fix = 9.0 / (2.0 + np.cos(wave * (FULL_TURN / length))) ** 2
    weight = fix * np.exp(-(math.pi**2) / EWALD_SPLIT**2 * fraction**2)
    return (fraction**2).astype(np.float32), weight.astype(np.float32)


def by_factor(value, angle):
    cosine, sine = math.cos(angle), math.sin(angle)
    real, imag = value
    if abs(sine) < 1e-12 and cosine > 0.0:
        return value
    if abs(cosine) < 1e-12 and sine > 0.0:
        return imag, -real
    return real * cosine + imag * sine, imag * cosine - real * sine


def radix_two(values):
    count = len(values)
    if count == 1:
        return values
    even, odd = radix_two(values[0::2]), radix_two(values[1::2])
    odd = [by_factor(value, FULL_TURN * k / count) for k, value in enumerate(odd)]
    first = [(a[0] + b[0], a[1] + b[1]) for a, b in zip(even, odd)]
    return first + [(a[0] - b[0], a[1] - b[1]) for a, b in zip(even, odd)]


def leading_transform(parts):
    bricks = len(parts[0])
    length = ZDEV * bricks
    result = [None] * length
    for k in range(bricks):
        base = parts[0][k]
        one = by_factor(parts[1][k], FULL_TURN * k / length)
        two = by_factor(parts[2][k], FULL_TURN * 2 * k / length)
        total = (one[0] + two[0], one[1] + two[1])
        apart = ((one[0] - two[0]) * (0.5 * math.sqrt(3.0)), (one[1] - two[1]) * (0.5 * math.sqrt(3.0)))
        middle = (base[0] - 0.5 * total[0], base[1] - 0.5 * total[1])
        result[k] = (base[0] + total[0], base[1] + total[1])
        result[k + bricks] = (middle[0] + apart[1], middle[1] - apart[0])
        result[k + 2 * bricks] = (middle[0] - apart[1], middle[1] + apart[0])
    return result


def fused_kernel(
    pencils, bricks,
    grid_ref, high_ref, low_ref, yterm_ref, xterm_ref,
    energy_ref, spectrum_ref,
    xs, xr, ys, zr, xs0, xr0, ys0, zr0, zd, ep, eb,
    xsend, xrecv, zsend, zrecv, xsend0, xrecv0, zsend0, zrecv0, epsend, eprecv, ebsend, ebrecv,
):
    mine = {"pencil": lax.axis_index("pencil"), "brick": lax.axis_index("brick")}
    sizes = {"pencil": pencils, "brick": bricks}
    part = NY // bricks
    rows = NY // pencils
    started = []

    def peer(axis, step):
        half = sizes[axis] // 2
        side, place = mine[axis] // half, mine[axis] % half
        if step <= half:
            return (1 - side) * half + lax.rem(place + step - 1, half)
        return side * half + lax.rem(place + step - half, half)

    def send(axis, step, source, target, send_sem, recv_sem):
        copy = pltpu.make_async_remote_copy(
            src_ref=source, dst_ref=target, send_sem=send_sem, recv_sem=recv_sem,
            device_id={axis: peer(axis, step)}, device_id_type=pl.DeviceIdType.MESH,
        )
        copy.start()
        started.append(copy)

    def arrived(axis, step, target, recv_sem, send_sem):
        pltpu.make_async_remote_copy(
            src_ref=target, dst_ref=target, send_sem=send_sem, recv_sem=recv_sem,
            device_id={axis: peer(axis, step)}, device_id_type=pl.DeviceIdType.MESH,
        ).wait_recv()

    barrier = pltpu.get_barrier_semaphore()
    for axis in sizes:
        for step in range(1, sizes[axis]):
            pl.semaphore_signal(
                barrier, inc=1, device_id={axis: peer(axis, step)},
                device_id_type=pl.DeviceIdType.MESH,
            )

    me, slab = mine["pencil"], mine["brick"]

    half = LANES // 2

    def send_first(part_index):
        for step in range(1, pencils):
            send(
                "pencil", step, xs0.at[part_index, peer("pencil", step)], xr0.at[part_index, me],
                xsend0.at[part_index, step], xrecv0.at[part_index, me],
            )

    def in_halves(real, imag):
        low = lax.broadcasted_iota(jnp.int32, real.shape, 1) < half
        return (
            jnp.where(low, real, pltpu.roll(imag, half, 1)),
            jnp.where(low, pltpu.roll(real, half, 1), imag),
        )

    def send_lines(plane):
        for step in range(1, pencils):
            send(
                "pencil", step, xs.at[plane, peer("pencil", step)], xr.at[plane, me],
                xsend.at[plane, step], xrecv.at[plane, me],
            )

    for plane in range(ZDEV):
        lines = jnp.concatenate([grid_ref[t, plane] for t in range(NX // LANES)], axis=1)
        lines = split(lines)
        real = dot3(lines, (high_ref[0:NX], low_ref[0:NX]), ((1,), (0,)))
        imag = -dot3(lines, (high_ref[NX:], low_ref[NX:]), ((1,), (0,)))
        if plane == 0:
            for target in range(pencils):
                own = slice(target * LANES, (target + 1) * LANES)
                xs0[0, target], xs0[1, target] = in_halves(real[:, own], imag[:, own])
            pl.semaphore_wait(barrier, pencils + bricks - 2)
            send_first(0)
            send_first(1)
            xr0[0, me] = xs0[0, me]
            xr0[1, me] = xs0[1, me]
            continue
        for target in range(pencils):
            xs[plane - 1, target, :, 0:LANES] = real[:, target * LANES : (target + 1) * LANES]
            xs[plane - 1, target, :, LANES:] = imag[:, target * LANES : (target + 1) * LANES]
        xr[plane - 1, me] = xs[plane - 1, me]

    def gathered(held):
        pieces = []
        for source in range(pencils):
            pieces.append(held[source, RIM:rows])
            pieces.append(held[source, rows : rows + RIM] + held[(source + 1) % pencils, 0:RIM])
        return split(jnp.concatenate(pieces, axis=0))

    for index in range(2):
        for step in range(1, pencils):
            other = peer("pencil", step)
            arrived(
                "pencil", step, xr0.at[index, other], xrecv0.at[index, other], xsend0.at[index, step]
            )
        send_lines(index)
        both = dot3((high_ref[...], low_ref[...]), gathered(xr0.at[index]), ((1,), (0,)))
        turned = pltpu.roll(both[NY:], half, 1)
        low = lax.broadcasted_iota(jnp.int32, turned.shape, 1) < half
        both = both[:NY] + jnp.where(low, turned, -turned)
        for target in range(bricks):
            ys0[index, target] = both[target * part : (target + 1) * part]
        for step in range(1, bricks):
            send(
                "brick", step, ys0.at[index, peer("brick", step)], zr0.at[index, slab],
                zsend0.at[index, step], zrecv0.at[index, slab],
            )
        zr0[index, slab] = ys0[index, slab]

    for plane in range(ZDEV - 1):
        for step in range(1, pencils):
            other = peer("pencil", step)
            arrived("pencil", step, xr.at[plane, other], xrecv.at[plane, other], xsend.at[plane, step])
        columns = gathered(xr.at[plane])
        both = dot3((high_ref[...], low_ref[...]), columns, ((1,), (0,)))
        real = both[:NY, :LANES] + both[NY:, LANES:]
        imag = both[:NY, LANES:] - both[NY:, :LANES]
        for target in range(bricks):
            ys[plane, target, :, 0:LANES] = real[target * part : (target + 1) * part]
            ys[plane, target, :, LANES:] = imag[target * part : (target + 1) * part]
        for step in range(1, bricks):
            send(
                "brick", step, ys.at[plane, peer("brick", step)], zr.at[plane, slab],
                zsend.at[plane, step], zrecv.at[plane, slab],
            )
        zr[plane, slab] = ys[plane, slab]

    def over_bricks(plane, step, carry):
        here = pl.ds(pl.multiple_of(step * 8, 8), 8)
        if plane == 0:
            values = [in_halves(zr0[0, b, here, :], zr0[1, b, here, :]) for b in range(bricks)]
        else:
            values = [
                (zr[0, b, here, 0:LANES], zr[0, b, here, LANES : 2 * LANES]) for b in range(bricks)
            ]
        for k, (real, imag) in enumerate(radix_two(values)):
            zd[plane, k, here, 0:LANES] = real
            zd[plane, k, here, LANES : 2 * LANES] = imag
        return carry

    for index in range(2):
        for step in range(1, bricks):
            other = peer("brick", step)
            arrived(
                "brick", step, zr0.at[index, other], zrecv0.at[index, other], zsend0.at[index, step]
            )
    for plane in range(ZDEV):
        if plane > 0:
            for step in range(1, bricks):
                other = peer("brick", step)
                arrived(
                    "brick", step, zr.at[plane - 1, other], zrecv.at[plane - 1, other],
                    zsend.at[plane - 1, step],
                )
        if plane + 1 < ZDEV:
            lax.fori_loop(0, part // 8, functools.partial(over_bricks, plane), 0)

    length = ZDEV * bricks
    depth_square, depth_weight = wave_terms(length)
    lanes = pl.ds(pl.multiple_of(me * LANES, LANES), LANES)

    def chunk(step, total):
        here = pl.ds(pl.multiple_of(step * 8, 8), 8)
        planes = [
            [(held[i, b, here, 0:LANES], held[i, b, here, LANES : 2 * LANES]) for b in range(bricks)]
            for held, i in ((zd, 0), (zd, 1), (zr, 1))
        ]
        result = leading_transform(planes[:-1] + [radix_two(planes[-1])])
        across = pl.ds(pl.multiple_of(slab * part + step * 8, 8), 8)
        square = yterm_ref[0, across, :] + xterm_ref[0, :, lanes]
        weight = yterm_ref[1, across, :] * xterm_ref[1, :, lanes]
        powers = {}
        for k, (real, imag) in enumerate(result):
            spectrum_ref[0, k, here, :] = real
            spectrum_ref[1, k, here, :] = imag
            fold = min(k, length - k)
            powers[fold] = powers.get(fold, 0.0) + (real * real + imag * imag)
        inner = jnp.zeros_like(total)
        for k, power in powers.items():
            q = square + float(depth_square[k])
            term = float(depth_weight[k]) * power / jnp.where(q == 0.0, 1.0, q)
            inner = inner + (jnp.where(q == 0.0, 0.0, term) if k == 0 else term)
        return total + inner * weight

    share = lax.fori_loop(0, part // 8, chunk, jnp.zeros((8, LANES), jnp.float32))
    share = share * (1.0 / (math.pi * (length * NY * NX)))
    for axis, held, sends, recvs in (
        ("pencil", ep, epsend, eprecv), ("brick", eb, ebsend, ebrecv),
    ):
        own = mine[axis]
        held[own] = share
        for step in range(1, sizes[axis]):
            send(axis, step, held.at[own], held.at[own], sends.at[step], recvs.at[own])
        for step in range(1, sizes[axis]):
            other = peer(axis, step)
            arrived(axis, step, held.at[other], recvs.at[other], sends.at[step])
        share = held[0]
        for source in range(1, sizes[axis]):
            share = share + held[source]
    energy_ref[...] = share
    for copy in started:
        copy.wait_send()


def transform_fused(grid, rows):
    pencils, bricks = lax.axis_size("pencil"), lax.axis_size("brick")
    part = NY // bricks
    columns = NX // pencils
    cosine, sine = tables(NY)
    turn_y = np.concatenate([cosine, sine], axis=0)

    def halves(table):
        high = table.astype(jnp.bfloat16)
        return high, (table - high.astype(np.float32)).astype(jnp.bfloat16)

    y_terms = np.broadcast_to(np.stack(wave_terms(NY))[:, :, None], (2, NY, LANES))
    x_terms = np.broadcast_to(np.stack(wave_terms(NX))[:, None, :], (2, 8, NX))
    f32 = jnp.float32
    whole = pl.BlockSpec(memory_space=pltpu.VMEM)
    dma = pltpu.SemaphoreType.DMA
    energy, spectrum = pl.pallas_call(
        functools.partial(fused_kernel, pencils, bricks),
        out_shape=(
            jax.ShapeDtypeStruct((8, LANES), f32),
            jax.ShapeDtypeStruct((2, ZDEV * bricks, part, columns), f32),
        ),
        in_specs=[whole] * 5,
        out_specs=(whole, whole),
        scratch_shapes=[
            pltpu.VMEM((ZDEV - 1, pencils, rows + RIM, 2 * LANES), f32),
            pltpu.VMEM((ZDEV - 1, pencils, rows + RIM, 2 * LANES), f32),
            pltpu.VMEM((ZDEV - 1, bricks, part, 2 * LANES), f32),
            pltpu.VMEM((ZDEV - 1, bricks, part, 2 * LANES), f32),
            pltpu.VMEM((2, pencils, rows + RIM, LANES), f32),
            pltpu.VMEM((2, pencils, rows + RIM, LANES), f32),
            pltpu.VMEM((2, bricks, part, LANES), f32),
            pltpu.VMEM((2, bricks, part, LANES), f32),
            pltpu.VMEM((2, bricks, part, 2 * LANES), f32),
            pltpu.VMEM((pencils, 8, LANES), f32),
            pltpu.VMEM((bricks, 8, LANES), f32),
            dma((ZDEV, pencils)), dma((ZDEV, pencils)),
            dma((ZDEV, bricks)), dma((ZDEV, bricks)),
            dma((2, pencils)), dma((2, pencils)),
            dma((2, bricks)), dma((2, bricks)),
            dma((pencils,)), dma((pencils,)), dma((bricks,)), dma((bricks,)),
        ],
        compiler_params=pltpu.CompilerParams(
            collective_id=0, has_side_effects=True, vmem_limit_bytes=24 * 1024 * 1024
        ),
        cost_estimate=pl.CostEstimate(
            flops=6_000_000_000, bytes_accessed=8_000_000, transcendentals=0
        ),
    )(grid, *halves(turn_y), y_terms.astype(np.float32), x_terms.astype(np.float32))
    return jnp.sum(energy).reshape(1), spectrum


def shards(positions, charges, anchor_row, anchor_column, counts):
    slot_count = anchor_row.shape[0]
    atoms = charges.shape[0]
    rows = NY // lax.axis_size("pencil")
    coords = jnp.concatenate([positions, charges.reshape(1, atoms)], axis=0)
    anchors = jnp.concatenate([anchor_row, anchor_column, counts])
    far_anchors, far_coords = (from_behind(array, "brick", -1) for array in (anchors, coords))
    grid = spread(3, rows, anchors, coords)
    grid = spread(0, rows, far_anchors, far_coords, grid)
    bricks = lax.axis_size("brick")
    tiled = NX // lax.axis_size("pencil") == LANES and NY // bricks % 8 == 0
    if tiled and bricks & (bricks - 1) == 0:
        total, spectrum = transform_fused(grid, rows)
    else:
        total, spectrum = transform_by_steps(grid, rows)
    slot_total = slot_count * lax.axis_size("brick") * lax.axis_size("pencil")
    return (total * (0.5 / slot_total), spectrum)


def solution(mesh):
    return jax.shard_map(
        shards,
        mesh=mesh,
        in_specs=(
            P(None, ("brick", "pencil")),
            P(("brick", "pencil")),
            P(("brick", "pencil")),
            P(("brick", "pencil")),
            P(("brick", "pencil")),
        ),
        out_specs=(P(), P(None, None, "brick", "pencil")),
        check_vma=False,
    )
```
